32 devices in a mesh: groups: 2 (over y), tile: 8 (over z, x), cuts: 2 (over core).
Axes of the slice: x: 2, y: 2, z: 4, core: 2. Of those that a mesh axis runs over, the one named last changes fastest.
Arguments:
- slice_rows: float32 [8192, 512], P(('groups', 'tile', 'cuts')), parts along dimension 0, may hold values from -0.025625 to 0.025625
- row_owner: int32 [8192, 1], P(('groups', 'tile', 'cuts')), parts along dimension 0, may hold values from 0 to 7; in each aligned block of 256 rows (0 to 255, 256 to 511, ...) at most 48 rows name the same one
- leaf_row: int32 [8192], P(('groups', 'tile', 'cuts')), parts along dimension 0, may hold values from 0 to 511
- exponent: int32 [8192], P(('groups', 'tile', 'cuts')), parts along dimension 0, may hold values from -1 to 1
- environment: float32 [16384, 512], P(('groups', 'tile', 'cuts')), parts along dimension 0, may hold values from -0.25 to 0.25
- ordering: int32 [32, 512], P(('groups', 'tile', 'cuts')), parts along dimension 0, may hold values from 0 to 511, each once within a row
- sign_mask: int32 [32, 512], P(('groups', 'tile', 'cuts')), parts along dimension 0, may hold values 0 or 1
Outputs:
- partition: float32 [1024, 512], P(('groups', 'tile'), 'cuts'), parts along dimension 0
- log_scale: float32 [2], P('groups'), parts along dimension 0
The draws below stay inside these ranges and needn't reach their ends.
There are 2 independent parts, one for each index of `groups`. The reference program is written for one: setup_inputs(seed, part) draws one part's arguments, and reference() takes and returns one part's arrays. A program takes and returns all parts, laid end to end along the dimension named above; each array names one. Nothing has to cross between parts.
Inputs may be any that keep to these rules, and one draw needn't show every extreme that they name: `row_owner`: of the rows of one device at most 48 name the same owner, and in some device exactly 48 do.
All inputs are finite; a program needn't handle non-finite values. No bound on the sum of `sign_mask` on one device may be relied on, other than what follows from the above.
Results may differ from the reference program's by a relative error of at most 0.0003.
Values sent between devices are 32-bit elements; how exact they have to be, the bound alone decides.
A program may use at most 64 MiB of HBM per device.

```python
import math
import jax
import jax.numpy as jnp
import numpy as np
from jax import lax

W = 512
ROWS_DEV = 256
CAP = 48
LEAVES = 16
ROWS = 4096
N_TILE = 8
N_CUTS = 2


def place_ends(result, own_key, smallest, top_value):
    longest = result.shape.index(max(result.shape))
    spots = []
    for shift in (0, 1):
        where = [jax.random.randint(jax.random.fold_in(own_key, axis), (), 0, length) for axis, length in enumerate(result.shape)]
        where[longest] = (where[longest] + shift) % result.shape[longest]
        spots.append(tuple(where))
    return result.at[spots[0]].set(smallest).at[spots[1]].set(top_value)


def steps_of(key, dims, shards, low, top_value):
    factor_of = 1.0
    for position, parts in shards:
        draws = jax.random.uniform(jax.random.fold_in(jax.random.fold_in(key, 6), position), (parts,), jnp.float32, low / len(shards), top_value / len(shards))
        factor_of = factor_of * jnp.repeat(jnp.exp(draws), dims[position] // parts).reshape((-1,) + (1,) * (len(dims) - 1 - position))
    return factor_of


def deal_out(own_key, own, number, rows, amount, top, bound, lean):
    sequence = jax.random.permutation(own_key, amount)
    crowded, usual = portions_of(amount, rows * top, bound, lean, True), portions_of(amount, rows * top, bound, lean, False)
    places = jnp.arange(amount)

    def named(tallies, turn):
        used = int((tallies > 0).sum())
        fixed = max(1, used // 4)
        shifted = fixed + (places - fixed + turn * (used - fixed)) % max(1, amount - fixed)
        return jnp.zeros((amount,), jnp.int32).at[sequence[jnp.where(places < fixed, places, shifted)]].set(jnp.asarray(tallies, jnp.int32))

    tallies = jnp.where(number % 4 == 0, named(crowded, number // 4), named(usual, number - number // 4 - 1))
    mixed = jax.random.permutation(jax.random.fold_in(own, 3), amount)
    giver, sink = mixed[0:amount // 2 * 2:2], mixed[1:amount // 2 * 2:2]
    room = jnp.minimum(tallies[giver] - 1, bound - tallies[sink]) // 2
    room = jnp.where((giver == sequence[0]) | (sink == sequence[0]) | (tallies[sink] == 0), 0, jnp.maximum(room, 0))
    shifted = jax.random.randint(jax.random.fold_in(own, 4), (amount // 2,), 0, 1 << 20) % (room + 1)
    tallies = tallies.at[giver].add(-shifted).at[sink].add(shifted)
    labels = jnp.searchsorted(jnp.cumsum(tallies), jnp.arange(rows * top), side="right").astype(jnp.int32)
    listing = labels.reshape(top, rows).T
    listing = listing[jax.random.permutation(jax.random.fold_in(own, 1), rows)]
    turn = jax.random.randint(jax.random.fold_in(own, 2), (rows, 1), 0, top)
    return jnp.take_along_axis(listing, (jnp.arange(top)[None, :] + turn) % top, axis=1)


def portions_of(count, total, limit, lean, full):
    portions = [(1 << 20) // math.isqrt(grade ** lean) + 1 for grade in range(1, count + 1)]
    largest = limit if full else min(limit, max(-(-total // count), total * portions[0] // sum(portions)))
    least = 1 if total - largest >= count - 1 else 0
    given, spare = [largest] + [least] * (count - 1), total - largest - least * (count - 1)
    while spare > 0:
        free = [i for i in range(1, count) if given[i] < largest] or [i for i in range(1, count) if given[i] < limit]
        whole, left = sum([portions[i] for i in free]), spare
        for i in free:
            extra = min(limit - given[i], max(1, left * portions[i] // whole), spare)
            given[i] = given[i] + extra
            spare = spare - extra
    return np.array(given)


def normal_values(rng, extent, scale, bound, pieces=(), held_as=jnp.bfloat16):
    result = scale * jax.random.normal(rng, extent, jnp.float32)
    if pieces:
        result = result * steps_of(rng, extent, pieces, -0.22, 0.18)
    return jnp.clip(result, -bound, bound).astype(held_as)


def setup_inputs(seed: int = 0, part: int = 0) -> dict:
    arg_keys = jax.random.split(jax.random.key(seed), 8)
    own_keys = jax.random.split(jax.random.fold_in(arg_keys[7], part), 8)
    slice_rows = normal_values(own_keys[0], (ROWS, W), (0.068 / ROWS_DEV ** 0.5), 0.025625, ((0, 16),), jnp.float32)
    row_owner_keys = jax.random.split(jax.random.fold_in(own_keys[1], 1), ROWS // ROWS_DEV)
    row_owner_turns = jax.random.permutation(jax.random.fold_in(own_keys[1], 3), ROWS // ROWS_DEV)
    row_owner = jax.vmap(lambda own, number: deal_out(jax.random.fold_in(own_keys[1], 2), own, number, ROWS_DEV, N_TILE, 1, CAP, 2))(row_owner_keys, row_owner_turns).reshape((ROWS, 1))
    leaf_row = place_ends(jax.random.randint(own_keys[2], (ROWS,), 0, W), jax.random.fold_in(own_keys[2], 1), 0, W - 1).astype(jnp.int32)
    exponent = place_ends(jax.random.randint(own_keys[3], (ROWS,), -1, 2), jax.random.fold_in(own_keys[3], 1), -1, 1).astype(jnp.int32)
    environment = normal_values(own_keys[4], (LEAVES * W, W), W ** -0.5, 0.25, ((0, 16),), jnp.float32)
    ordering = jax.vmap(lambda own: jax.random.permutation(own, W))(jax.random.split(own_keys[5], LEAVES)).reshape((LEAVES, W)).astype(jnp.int32)
    sign_mask = place_ends((jax.random.randint(own_keys[6], (LEAVES, W), 0, 2) < 1).astype(jnp.int32), jax.random.fold_in(own_keys[6], 1), 0, 1)
    return {"slice_rows": slice_rows, "row_owner": row_owner, "leaf_row": leaf_row, "exponent": exponent, "environment": environment, "ordering": ordering, "sign_mask": sign_mask}


def reference(slice_rows, row_owner, leaf_row, exponent, environment, ordering, sign_mask):
    leaves = N_TILE * N_CUTS
    width = slice_rows.shape[1]
    source = jnp.arange(slice_rows.shape[0], dtype=jnp.int32) // ROWS_DEV
    target = (row_owner[:, 0] * N_CUTS + source % N_CUTS).astype(jnp.int32)
    factor = jnp.where(exponent == -1, 0.5, jnp.where(exponent == 1, 2.0, 1.0)).astype(jnp.float32)
    scaled = slice_rows * factor[:, None]
    collected = jnp.zeros((leaves, width, width), jnp.float32).at[target, leaf_row].add(scaled)
    environ = environment.reshape(leaves, width, width)
    columns = jnp.arange(width, dtype=jnp.int32)

    def advance(product, ordinal):
        device = ordinal % N_TILE * N_CUTS + ordinal // N_TILE
        contracted = jnp.dot(collected[device], environ[device], precision=lax.Precision.HIGHEST, preferred_element_type=jnp.float32)
        signs = 1.0 - 2.0 * sign_mask[device].astype(jnp.float32)
        signed = (ordering[device][:, None] == columns[None, :]).astype(jnp.float32) * signs[:, None]
        leaf = contracted + signed
        return (jnp.dot(product, leaf, precision=lax.Precision.HIGHEST, preferred_element_type=jnp.float32), None)
    product, _ = lax.scan(advance, jnp.eye(width, dtype=jnp.float32), jnp.arange(leaves, dtype=jnp.int32))
    spread = jnp.sqrt(jnp.mean(product * product) + 1e-06)
    return (product / spread, jnp.log(spread).reshape(1))
```

```python
import functools

import jax
import jax.numpy as jnp
from jax import lax
from jax.experimental import pallas as pl
from jax.experimental.pallas import tpu as pltpu
from jax.sharding import PartitionSpec as P

MESH = pl.DeviceIdType.MESH
F32, BF16 = jnp.float32, jnp.bfloat16
NN = (((1,), (0,)), ((), ()))
NT = (((1,), (1,)), ((), ()))


def halves(x):
    high = x.astype(BF16)
    return high, (x - high.astype(F32)).astype(BF16)


def dot(a, b, dims=NN):
    return lax.dot_general(a, b, dims, preferred_element_type=F32)


def dot3(left, right, dims=NN):
    return (dot(left[0], right[1], dims) + dot(left[1], right[0], dims)) + dot(left[0], right[0], dims)


def kernel(tiles, cap,
           rows_ref, owner_ref, leaf_row_ref, exponent_ref, env_ref, ordering_ref, sign_ref,
           block_ref, square_ref,
           out_rows, out_ids, in_rows, in_ids, own, own_high, own_low, chain_high, chain_low,
           pair_in, chain_in, chain_out, p_in, q_in, sums_out, sums_in,
           route_send, route_recv, pair_send, pair_recv, chain_send, chain_recv,
           p_send, p_recv, pass_send, pass_recv, q_send, q_recv, half_send, sum_send, sum_recv):
    group, me, cut = lax.axis_index("groups"), lax.axis_index("tile"), lax.axis_index("cuts")
    rows, width = rows_ref.shape
    step = width // tiles
    half = tiles // 2
    slots = tiles * cap
    count = 2 * tiles
    ident = me * 2 + cut
    place = jnp.where(cut == 0, me, tiles - 1 - me)
    way = 1 - 2 * cut
    last = place == tiles - 1

    def chunk(ref, k):
        return ref.at[pl.ds(pl.multiple_of(k * step, 8), step)]

    def remote(src, dst, send, recv, tile, other):
        return pltpu.make_async_remote_copy(
            src_ref=src, dst_ref=dst, send_sem=send, recv_sem=recv,
            device_id=(group, tile, other), device_id_type=MESH)

    barrier = pltpu.get_barrier_semaphore()

    @pl.loop(1, count)
    def _(d):
        peer = lax.rem(ident + d, count)
        pl.semaphore_signal(barrier, inc=1, device_id=(group, peer // 2, lax.rem(peer, 2)), device_id_type=MESH)

    square = 128 * ((rows + 127) // 128)
    level = exponent_ref[...]
    factor = jnp.where(level == -1, 0.5, jnp.where(level == 1, 2.0, 1.0)).astype(F32)
    factor = jnp.broadcast_to(factor, (128, rows)).T[:, 0:1]
    scaled = rows_ref[...] * factor
    owner = owner_ref[...]
    hits = (owner == lax.broadcasted_iota(jnp.int32, (rows, 128), 1)).astype(F32)
    earlier = (lax.broadcasted_iota(jnp.int32, (rows, rows), 1)
               < lax.broadcasted_iota(jnp.int32, (rows, rows), 0)).astype(F32)
    before = dot(earlier.astype(BF16), hits.astype(BF16))
    position = jnp.sum(before * hits, axis=1, keepdims=True)
    position = jnp.broadcast_to(position, (rows, 128)).T[0:1, :].astype(jnp.int32)
    owner = jnp.broadcast_to(owner.astype(F32), (rows, 128)).T[0:1, :].astype(jnp.int32)
    slot = lax.broadcasted_iota(jnp.int32, (slots, rows), 0)
    pick = (slot == owner * cap + position).astype(F32).astype(BF16)
    high = scaled.astype(BF16)
    rest = scaled - high.astype(F32)
    middle = rest.astype(BF16)
    low = (rest - middle.astype(F32)).astype(BF16)
    out_rows[...] = (dot(pick, low) + dot(pick, middle)) + dot(pick, high)
    seat = (slot == me * cap + position).astype(F32).astype(BF16)
    named = jnp.where(lax.broadcasted_iota(jnp.int32, (tiles, rows), 0) == owner,
                      leaf_row_ref[...] + 1, 0).astype(F32)
    named_high, named_low = halves(named)
    ids = dot(named_high, seat, NT) + dot(named_low, seat, NT)
    for t in range(tiles):
        out_ids[t] = ids[t:t + 1, :]

    pl.semaphore_wait(barrier, count - 1)

    def slots_of(ref, t):
        return ref.at[pl.ds(pl.multiple_of(t * cap, 8), cap)]

    def route(to, source):
        return (remote(slots_of(out_rows, to), slots_of(in_rows, source), route_send.at[0, to],
                       route_recv.at[0, source], to, cut),
                remote(out_ids.at[to], in_ids.at[source], route_send.at[1, to],
                       route_recv.at[1, source], to, cut))

    @pl.loop(1, tiles)
    def _(d):
        for copy in route(lax.rem(me + d, tiles), me):
            copy.start()

    mine = pl.ds(pl.multiple_of(me * cap, 8), cap)
    in_rows[mine] = out_rows[mine]
    in_ids[me] = out_ids[me]
    bond = jnp.where(lax.broadcasted_iota(jnp.int32, (width, width), 0) == ordering_ref[...],
                     (1 - 2 * sign_ref[...]).astype(F32), 0.0)

    @pl.when(cut == 0)
    def _():
        own[...] = bond.T
        own_high[...], own_low[...] = halves(env_ref[...])

    @pl.when(cut == 1)
    def _():
        own[...] = bond
        own_high[...], own_low[...] = halves(env_ref[...].T)

    @pl.loop(1, tiles)
    def _(d):
        source = lax.rem(me + d, tiles)
        for copy in route(source, source):
            copy.wait_recv()

    wanted = jnp.sum(in_ids[...], axis=0).astype(jnp.int32) - 1
    spread_out = (lax.broadcasted_iota(jnp.int32, (width, slots), 0) == wanted).astype(F32).astype(BF16)
    in_high, in_low = halves(in_rows[...])
    collected = halves(dot(spread_out, in_low) + dot(spread_out, in_high))

    @pl.when(cut == 0)
    def _():
        own[...] += dot3(collected, (own_high[...], own_low[...]))

    @pl.when(cut == 1)
    def _():
        own[...] += dot3((own_high[...], own_low[...]), collected, NT)

    def pair(k):
        return remote(chunk(own, k), chunk(pair_in, k), pair_send.at[k], pair_recv.at[k], me + way, cut)

    def link(k):
        return remote(chunk(chain_out, k), chunk(chain_in, k), chain_send.at[k], chain_recv.at[k],
                      lax.rem(me + 2 * way + tiles, tiles), cut)

    def p_copy(k):
        return remote(chunk(chain_out, k), p_in, p_send.at[k], p_recv.at[0], k, 0)

    def q_along(k):
        return remote(chunk(q_in, k), chunk(q_in, k), q_send.at[0, k], q_recv.at[k], lax.rem(me + 2, tiles), cut)

    def q_across(k):
        return remote(chunk(q_in, k), chunk(q_in, k), q_send.at[1, k], q_recv.at[k], lax.rem(me + 1, tiles), cut)

    def q_half(k):
        return remote(chunk(chain_out, k), chunk(q_in, k), half_send.at[k], q_recv.at[k], 0, 0)

    even_tile = lax.rem(me, 2) == 0
    even_place = lax.rem(place, 2) == 0
    p_root = jnp.logical_and(last, cut == 0)
    q_root = jnp.logical_and(last, cut == 1)

    def emit(k, value):
        at = pl.ds(pl.multiple_of(k * step, 8), step)

        @pl.when(jnp.logical_not(last))
        def _():
            chain_out[at] = value
            link(k).start()

        @pl.when(p_root)
        def _():
            @pl.when(k < tiles - 1)
            def _():
                chain_out[at] = value
                p_copy(k).start()

            @pl.when(k == tiles - 1)
            def _():
                p_in[...] = value

        @pl.when(q_root)
        def _():
            @pl.when(k < half)
            def _():
                chain_out[at] = value
                q_half(k).start()

            @pl.when(k >= half)
            def _():
                q_in[pl.ds(pl.multiple_of((k - half) * step, 8), step)] = value
                q_along(k - half).start()
                q_across(k - half).start()

    @pl.when(even_place)
    def _():
        @pl.loop(0, tiles)
        def _(k):
            pair(k).start()

    @pl.when(jnp.logical_not(even_place))
    def _():
        own_high[...], own_low[...] = halves(own[...])

        @pl.loop(0, tiles)
        def _(k):
            at = pl.ds(pl.multiple_of(k * step, 8), step)
            pair(k).wait_recv()
            value = dot3(halves(pair_in[at]), (own_high[...], own_low[...]))

            @pl.when(place == 1)
            def _():
                emit(k, value)

            @pl.when(place > 1)
            def _():
                chain_high[at], chain_low[at] = halves(value)

        @pl.when(place > 1)
        def _():
            @pl.loop(0, tiles)
            def _(k):
                at = pl.ds(pl.multiple_of(k * step, 8), step)
                link(k).wait_recv()
                emit(k, dot3(halves(chain_in[at]), (chain_high[...], chain_low[...])))

    @pl.when(jnp.logical_not(q_root))
    def _():
        @pl.loop(0, half)
        def _(k):
            q_half(k).wait_recv()

            @pl.when(even_tile)
            def _():
                @pl.when(me < tiles - 2)
                def _():
                    q_along(k).start()

                q_across(k).start()

    def p_pass():
        return remote(p_in, p_in, pass_send.at[0], pass_recv.at[0], me, 1)

    @pl.when(cut == 0)
    def _():
        @pl.when(jnp.logical_not(p_root))
        def _():
            p_copy(0).wait_recv()

        p_pass().start()

    @pl.when(cut == 1)
    def _():
        p_pass().wait_recv()

    result = dot3(halves(p_in[...]), halves(q_in[...]), NT)
    block_ref[...] = result
    total = jnp.sum(jnp.sum(result * result, axis=0, keepdims=True), axis=1, keepdims=True)
    total = jnp.broadcast_to(total, (8, 128))
    sums_out[...] = total

    def share(peer, slot):
        return remote(sums_out, sums_in.at[slot], sum_send.at[peer], sum_recv.at[slot],
                      peer // 2, lax.rem(peer, 2))

    @pl.loop(1, count)
    def _(d):
        share(lax.rem(ident + d, count), ident).start()

    sums_in[ident] = total

    @pl.loop(1, tiles)
    def _(d):
        for copy in route(lax.rem(me + d, tiles), me):
            copy.wait_send()

    @pl.when(even_place)
    def _():
        @pl.loop(0, tiles)
        def _(k):
            pair(k).wait_send()

    @pl.when(jnp.logical_and(jnp.logical_not(even_place), jnp.logical_not(last)))
    def _():
        @pl.loop(0, tiles)
        def _(k):
            link(k).wait_send()

    @pl.when(p_root)
    def _():
        @pl.loop(0, tiles - 1)
        def _(k):
            p_copy(k).wait_send()

    @pl.when(q_root)
    def _():
        @pl.loop(0, half)
        def _(k):
            q_half(k).wait_send()

    @pl.when(even_tile)
    def _():
        @pl.loop(0, half)
        def _(k):
            @pl.when(me < tiles - 2)
            def _():
                q_along(k).wait_send()

            q_across(k).wait_send()

    @pl.when(cut == 0)
    def _():
        p_pass().wait_send()

    @pl.loop(1, count)
    def _(d):
        peer = lax.rem(ident + d, count)
        share(peer, peer).wait_recv()
        share(peer, peer).wait_send()

    square_ref[...] = jnp.sum(sums_in[...], axis=0)


def body(slice_rows, row_owner, leaf_row, exponent, environment, ordering, sign_mask):
    tiles = lax.axis_size("tile")
    rows, width = slice_rows.shape
    step = width // tiles
    half = width // 2
    cap = max(2, (3 * rows + 2 * tiles - 1) // (2 * tiles))
    cap = (cap + 15) // 16 * 16
    slots = tiles * cap
    count = 2 * tiles
    vmem, dma = pltpu.VMEM, pltpu.SemaphoreType.DMA
    block, square = pl.pallas_call(
        functools.partial(kernel, tiles, cap),
        out_shape=(jax.ShapeDtypeStruct((step, half), F32), jax.ShapeDtypeStruct((8, 128), F32)),
        in_specs=[pl.BlockSpec(memory_space=vmem)] * 7,
        out_specs=(pl.BlockSpec(memory_space=vmem), pl.BlockSpec(memory_space=vmem)),
        scratch_shapes=[
            vmem((slots, width), F32), vmem((tiles, 1, slots), F32),
            vmem((slots, width), F32), vmem((tiles, 1, slots), F32),
            vmem((width, width), F32), vmem((width, width), BF16), vmem((width, width), BF16),
            vmem((width, width), BF16), vmem((width, width), BF16),
            vmem((width, width), F32), vmem((width, width), F32), vmem((width, width), F32),
            vmem((step, width), F32), vmem((half, width), F32),
            vmem((8, 128), F32), vmem((count, 8, 128), F32),
            dma((2, tiles)), dma((2, tiles)), dma((tiles,)), dma((tiles,)), dma((tiles,)), dma((tiles,)),
            dma((tiles,)), dma((1,)), dma((1,)), dma((1,)),
            dma((2, tiles // 2)), dma((tiles // 2,)), dma((tiles // 2,)), dma((count,)), dma((count,)),
        ],
        compiler_params=pltpu.CompilerParams(
            collective_id=0, has_side_effects=True, vmem_limit_bytes=40 * 1024 * 1024),
    )(slice_rows, row_owner, leaf_row.reshape(1, rows), exponent.reshape(1, rows),
      environment, ordering, sign_mask)
    spread = jnp.sqrt(square[0, 0] / (width * width) + 1e-06)
    return block / spread, jnp.log(spread).reshape(1)


def from_partner(x, axis, bit):
    return lax.ppermute(x, axis, [(i, i ^ 1 << bit) for i in range(lax.axis_size(axis))])


def multiply(left_factor, right_factor):
    return jnp.dot(
        left_factor,
        right_factor,
        precision=lax.Precision.HIGHEST,
        preferred_element_type=jnp.float32,
    )


def plain_body(slice_rows, row_owner, leaf_row, exponent, environment, ordering, sign_mask):
    tiles = lax.axis_size("tile")
    cut_count = lax.axis_size("cuts")
    width = slice_rows.shape[1]
    row_count = slice_rows.shape[0]
    capacity = max(2, (3 * row_count + 2 * tiles - 1) // (2 * tiles))
    factor = jnp.where(exponent == -1, 0.5, jnp.where(exponent == 1, 2.0, 1.0)).astype(jnp.float32)
    scaled = slice_rows * factor[:, None]
    owners = row_owner[:, 0]
    hits = (owners[:, None] == jnp.arange(tiles, dtype=jnp.int32)[None, :]).astype(jnp.int32)
    before = jnp.cumsum(hits, axis=0) - hits
    position = jnp.sum(before * hits, axis=1)
    placed = owners * capacity + position
    outgoing = jnp.zeros((tiles * capacity, width), jnp.float32).at[placed].set(scaled)
    outgoing_rows = jnp.zeros((tiles * capacity,), jnp.int32).at[placed].set(leaf_row)
    arrived, arrived_rows = (
        lax.all_to_all(outgoing, "tile", split_axis=0, concat_axis=0, tiled=True),
        lax.all_to_all(outgoing_rows, "tile", split_axis=0, concat_axis=0, tiled=True),
    )
    collected = jnp.zeros((width, width), jnp.float32).at[arrived_rows].add(arrived)
    contracted = multiply(collected, environment)
    columns = jnp.arange(width, dtype=jnp.int32)
    signs = 1.0 - 2.0 * sign_mask[0].astype(jnp.float32)
    signed = (ordering[0][:, None] == columns[None, :]).astype(jnp.float32) * signs[:, None]
    product = contracted + signed
    for level in range(tiles.bit_length() - 1):
        partner = from_partner(product, "tile", level)
        upper = lax.axis_index("tile") >> level & 1 == 1
        first_part = jnp.where(upper, partner, product)
        second_part = jnp.where(upper, product, partner)
        product = multiply(first_part, second_part)
    level = 0
    partner = from_partner(product, "cuts", level)
    upper = lax.axis_index("cuts") >> level & 1 == 1
    first_part = jnp.where(upper, partner, product)
    second_part = jnp.where(upper, product, partner)
    product = multiply(first_part, second_part)
    spread = jnp.sqrt(jnp.mean(product * product) + 1e-06)
    rows_each = width // tiles
    cols_each = width // cut_count
    row_start = lax.axis_index("tile") * rows_each
    col_start = lax.axis_index("cuts") * cols_each
    own_block = lax.dynamic_slice(product, (row_start, col_start), (rows_each, cols_each))
    return (own_block / spread, jnp.log(spread).reshape(1))


def solution(mesh):
    tiles, cuts = mesh.shape["tile"], mesh.shape["cuts"]
    fits = cuts == 2 and 4 <= tiles <= 16
    return jax.shard_map(
        body if fits else plain_body,
        mesh=mesh,
        in_specs=(
            P(("groups", "tile", "cuts"), None),
            P(("groups", "tile", "cuts"), None),
            P(("groups", "tile", "cuts")),
            P(("groups", "tile", "cuts")),
            P(("groups", "tile", "cuts"), None),
            P(("groups", "tile", "cuts"), None),
            P(("groups", "tile", "cuts"), None),
        ),
        out_specs=(P(("groups", "tile"), "cuts"), P("groups")),
        check_vma=False,
    )
```

```python
import functools

import jax
import jax.numpy as jnp
from jax import lax
from jax.experimental import pallas as pl
from jax.experimental.pallas import tpu as pltpu
from jax.sharding import PartitionSpec as P

MESH = pl.DeviceIdType.MESH
F32, BF16 = jnp.float32, jnp.bfloat16
NN = (((1,), (0,)), ((), ()))
NT = (((1,), (1,)), ((), ()))


def halves(x):
    high = x.astype(BF16)
    return high, (x - high.astype(F32)).astype(BF16)


def dot(a, b, dims=NN):
    return lax.dot_general(a, b, dims, preferred_element_type=F32)


def dot3(left, right, dims=NN):
    return (dot(left[0], right[1], dims) + dot(left[1], right[0], dims)) + dot(left[0], right[0], dims)


def kernel(tiles, cap, parts,
           rows_ref, owner_ref, leaf_row_ref, exponent_ref, env_ref, ordering_ref, sign_ref,
           block_ref, square_ref,
           rows_in, env_in, out_rows, out_ids, in_rows, in_ids, bond_out, bond_in, env_out, env_far,
           own, far, own_high, own_low, chain_high, chain_low,
           chain_in, chain_out, p_in, q_in, sums_out, sums_in,
           load, route_send, route_recv, far_send, far_recv, chain_send, chain_recv,
           p_send, p_recv, pass_send, pass_recv, q_send, q_recv, half_send, sum_send, sum_recv):
    group, me, cut = lax.axis_index("groups"), lax.axis_index("tile"), lax.axis_index("cuts")
    load_env = pltpu.make_async_copy(env_ref, env_in, load.at[0])
    load_rows = pltpu.make_async_copy(rows_ref, rows_in, load.at[1])
    load_env.start()
    load_rows.start()
    rows, width = rows_ref.shape
    step = width // tiles
    pairs = tiles // 2
    bits = pairs * parts
    bit_rows = step // parts
    slots = tiles * cap
    count = 2 * tiles
    ident = me * 2 + cut
    place = jnp.where(cut == 0, me, tiles - 1 - me)
    way = 1 - 2 * cut
    last = place == tiles - 1
    host = lax.rem(place, 2) == 1
    pair_me = me // 2

    def chunk(ref, k):
        return ref.at[pl.ds(pl.multiple_of(k * step, 8), step)]

    def part(ref, i):
        return ref.at[pl.ds(pl.multiple_of(i * bit_rows, 8), bit_rows)]

    def remote(src, dst, send, recv, tile, other):
        return pltpu.make_async_remote_copy(
            src_ref=src, dst_ref=dst, send_sem=send, recv_sem=recv,
            device_id=(group, tile, other), device_id_type=MESH)

    barrier = pltpu.get_barrier_semaphore()

    @pl.loop(1, count)
    def _(d):
        peer = lax.rem(ident + d, count)
        pl.semaphore_signal(barrier, inc=1, device_id=(group, peer // 2, lax.rem(peer, 2)), device_id_type=MESH)

    bond_out[0:1] = ordering_ref[...]
    bond_out[1:2] = sign_ref[...]
    load_env.wait()

    @pl.when(cut == 0)
    def _():
        env_out[...] = env_in[...]

    @pl.when(cut == 1)
    def _():
        env_out[...] = env_in[...].T

    def to_host():
        to = lax.rem(me + way + tiles, tiles)
        return (remote(bond_out, bond_in, far_send.at[0], far_recv.at[0], to, cut),
                remote(env_out, env_far, far_send.at[1], far_recv.at[1], to, cut))

    pl.semaphore_wait(barrier, count - 1)

    @pl.when(jnp.logical_not(host))
    def _():
        for copy in to_host():
            copy.start()

    load_rows.wait()
    level = exponent_ref[...]
    factor = jnp.where(level == -1, 0.5, jnp.where(level == 1, 2.0, 1.0)).astype(F32)
    factor = jnp.broadcast_to(factor, (128, rows)).T[:, 0:1]
    scaled = rows_in[...] * factor
    owner = owner_ref[...]
    hits = (owner == lax.broadcasted_iota(jnp.int32, (rows, 128), 1)).astype(F32)
    earlier = (lax.broadcasted_iota(jnp.int32, (rows, rows), 1)
               < lax.broadcasted_iota(jnp.int32, (rows, rows), 0)).astype(F32)
    before = dot(earlier.astype(BF16), hits.astype(BF16))
    position = jnp.sum(before * hits, axis=1, keepdims=True)
    position = jnp.broadcast_to(position, (rows, 128)).T[0:1, :].astype(jnp.int32)
    owner = jnp.broadcast_to(owner.astype(F32), (rows, 128)).T[0:1, :].astype(jnp.int32)
    slot = lax.broadcasted_iota(jnp.int32, (slots, rows), 0)
    pick = (slot == owner * cap + position).astype(F32).astype(BF16)
    high = scaled.astype(BF16)
    rest = scaled - high.astype(F32)
    middle = rest.astype(BF16)
    low = (rest - middle.astype(F32)).astype(BF16)
    out_rows[...] = ((dot(pick, low) + dot(pick, middle)) + dot(pick, high)).reshape(tiles, cap, width)
    seat = (slot == me * cap + position).astype(F32).astype(BF16)
    named = jnp.where(lax.broadcasted_iota(jnp.int32, (tiles, rows), 0) == owner,
                      leaf_row_ref[...] + 1, 0).astype(F32)
    named_high, named_low = halves(named)
    ids = dot(named_high, seat, NT) + dot(named_low, seat, NT)
    for t in range(tiles):
        out_ids[t] = ids[t:t + 1, :]

    def slots_of(source):
        return pl.ds(pl.multiple_of(source * cap, 8), cap)

    def route(pair, source):
        both = pl.ds(2 * pair, 2)
        to = 2 * pair + 1 - cut
        return (remote(out_rows.at[both], in_rows.at[:, slots_of(source)], route_send.at[0, pair],
                       route_recv.at[0, source], to, cut),
                remote(out_ids.at[both], in_ids.at[:, source], route_send.at[1, pair],
                       route_recv.at[1, source], to, cut))

    @pl.loop(1, pairs)
    def _(d):
        for copy in route(lax.rem(pair_me + d, pairs), me):
            copy.start()

    @pl.when(jnp.logical_not(host))
    def _():
        for copy in route(pair_me, me):
            copy.start()

    def bond_of(order, sign):
        return jnp.where(lax.broadcasted_iota(jnp.int32, (width, width), 0) == order,
                         (1 - 2 * sign).astype(F32), 0.0)

    @pl.when(host)
    def _():
        for c in range(2):
            in_rows[c, slots_of(me)] = out_rows[2 * pair_me + c]
            in_ids[c, me] = out_ids[2 * pair_me + c]
        to_host()[0].wait_recv()

        @pl.when(cut == 0)
        def _():
            own[...] = bond_of(bond_out[0:1], bond_out[1:2]).T
            far[...] = bond_of(bond_in[0:1], bond_in[1:2]).T

        @pl.when(cut == 1)
        def _():
            own[...] = bond_of(bond_out[0:1], bond_out[1:2])
            far[...] = bond_of(bond_in[0:1], bond_in[1:2])

        own_high[...], own_low[...] = halves(env_out[...])
        to_host()[1].wait_recv()
        chain_high[...], chain_low[...] = halves(env_far[...])

        @pl.loop(1, tiles)
        def _(d):
            source = lax.rem(me + d, tiles)
            for copy in route(pair_me, source):
                copy.wait_recv()

        def collected(c):
            wanted = jnp.sum(in_ids[c], axis=0).astype(jnp.int32) - 1
            spread_out = (lax.broadcasted_iota(jnp.int32, (width, slots), 0) == wanted).astype(F32).astype(BF16)
            in_high, in_low = halves(in_rows[c])
            return halves(dot(spread_out, in_low) + dot(spread_out, in_high))

        @pl.when(cut == 0)
        def _():
            own[...] += dot3(collected(1), (own_high[...], own_low[...]))
            far[...] += dot3(collected(0), (chain_high[...], chain_low[...]))

        @pl.when(cut == 1)
        def _():
            own[...] += dot3((own_high[...], own_low[...]), collected(0), NT)
            far[...] += dot3((chain_high[...], chain_low[...]), collected(1), NT)

        own_high[...], own_low[...] = halves(own[...])

    def link(k):
        return remote(chunk(chain_out, k), chunk(chain_in, k), chain_send.at[k], chain_recv.at[k],
                      lax.rem(me + 2 * way + tiles, tiles), cut)

    def p_copy(k):
        return remote(chunk(chain_out, k), p_in, p_send.at[k], p_recv.at[0], k, 0)

    def q_along(i):
        return remote(part(q_in, i), part(q_in, i), q_send.at[0, i], q_recv.at[i], lax.rem(me + 2, tiles), cut)

    def q_across(i):
        return remote(part(q_in, i), part(q_in, i), q_send.at[1, i], q_recv.at[i], lax.rem(me + 1, tiles), cut)

    def q_half(i):
        return remote(part(chain_out, i), part(q_in, i), half_send.at[i], q_recv.at[i], 0, 0)

    even_tile = lax.rem(me, 2) == 0
    p_root = jnp.logical_and(last, cut == 0)
    q_root = jnp.logical_and(last, cut == 1)

    def emit(k, value):
        at = pl.ds(pl.multiple_of(k * step, 8), step)

        @pl.when(jnp.logical_not(last))
        def _():
            chain_out[at] = value
            link(k).start()

        @pl.when(p_root)
        def _():
            @pl.when(k < tiles - 1)
            def _():
                chain_out[at] = value
                p_copy(k).start()

            @pl.when(k == tiles - 1)
            def _():
                p_in[...] = value

        @pl.when(q_root)
        def _():
            @pl.when(k < pairs)
            def _():
                chain_out[at] = value
                for i in range(parts):
                    q_half(k * parts + i).start()

            @pl.when(k >= pairs)
            def _():
                q_in[pl.ds(pl.multiple_of((k - pairs) * step, 8), step)] = value
                for i in range(parts):
                    q_along((k - pairs) * parts + i).start()
                    q_across((k - pairs) * parts + i).start()

    @pl.when(place == 1)
    def _():
        @pl.loop(0, tiles)
        def _(k):
            at = pl.ds(pl.multiple_of(k * step, 8), step)
            emit(k, dot3(halves(far[at]), (own_high[...], own_low[...])))

    @pl.when(jnp.logical_and(host, place > 1))
    def _():
        chain_high[...], chain_low[...] = halves(dot3(halves(far[...]), (own_high[...], own_low[...])))

        @pl.loop(0, tiles)
        def _(k):
            at = pl.ds(pl.multiple_of(k * step, 8), step)
            link(k).wait_recv()
            emit(k, dot3(halves(chain_in[at]), (chain_high[...], chain_low[...])))

    @pl.when(jnp.logical_not(q_root))
    def _():
        @pl.loop(0, bits)
        def _(k):
            q_half(k).wait_recv()

            @pl.when(even_tile)
            def _():
                @pl.when(me < tiles - 2)
                def _():
                    q_along(k).start()

                q_across(k).start()

    def p_pass():
        return remote(p_in, p_in, pass_send.at[0], pass_recv.at[0], me, 1)

    @pl.when(cut == 0)
    def _():
        @pl.when(jnp.logical_not(p_root))
        def _():
            p_copy(0).wait_recv()

        p_pass().start()

    @pl.when(cut == 1)
    def _():
        p_pass().wait_recv()

    result = dot3(halves(p_in[...]), halves(q_in[...]), NT)
    block_ref[...] = result
    total = jnp.sum(jnp.sum(result * result, axis=0, keepdims=True), axis=1, keepdims=True)
    total = jnp.broadcast_to(total, (8, 128))
    sums_out[...] = total

    def share(peer, slot):
        return remote(sums_out, sums_in.at[slot], sum_send.at[peer], sum_recv.at[slot],
                      peer // 2, lax.rem(peer, 2))

    @pl.loop(1, count)
    def _(d):
        share(lax.rem(ident + d, count), ident).start()

    sums_in[ident] = total

    @pl.loop(1, pairs)
    def _(d):
        for copy in route(lax.rem(pair_me + d, pairs), me):
            copy.wait_send()

    @pl.when(jnp.logical_not(host))
    def _():
        for copy in route(pair_me, me) + to_host():
            copy.wait_send()

    @pl.when(jnp.logical_and(host, jnp.logical_not(last)))
    def _():
        @pl.loop(0, tiles)
        def _(k):
            link(k).wait_send()

    @pl.when(p_root)
    def _():
        @pl.loop(0, tiles - 1)
        def _(k):
            p_copy(k).wait_send()

    @pl.when(q_root)
    def _():
        @pl.loop(0, bits)
        def _(k):
            q_half(k).wait_send()

    @pl.when(even_tile)
    def _():
        @pl.loop(0, bits)
        def _(k):
            @pl.when(me < tiles - 2)
            def _():
                q_along(k).wait_send()

            q_across(k).wait_send()

    @pl.when(cut == 0)
    def _():
        p_pass().wait_send()

    @pl.loop(1, count)
    def _(d):
        peer = lax.rem(ident + d, count)
        share(peer, peer).wait_recv()
        share(peer, peer).wait_send()

    square_ref[...] = jnp.sum(sums_in[...], axis=0)


def body(slice_rows, row_owner, leaf_row, exponent, environment, ordering, sign_mask):
    tiles = lax.axis_size("tile")
    rows, width = slice_rows.shape
    step = width // tiles
    half = width // 2
    cap = max(2, (3 * rows + 2 * tiles - 1) // (2 * tiles))
    cap = (cap + 15) // 16 * 16
    slots = tiles * cap
    count = 2 * tiles
    parts = 2 if step % 32 == 0 else 1
    bits = tiles // 2 * parts
    vmem, dma = pltpu.VMEM, pltpu.SemaphoreType.DMA
    block, square = pl.pallas_call(
        functools.partial(kernel, tiles, cap, parts),
        out_shape=(jax.ShapeDtypeStruct((step, half), F32), jax.ShapeDtypeStruct((8, 128), F32)),
        in_specs=[pl.BlockSpec(memory_space=pl.ANY if i in (0, 4) else vmem) for i in range(7)],
        out_specs=(pl.BlockSpec(memory_space=vmem), pl.BlockSpec(memory_space=vmem)),
        scratch_shapes=[
            vmem((rows, width), F32), vmem((width, width), F32),
            vmem((tiles, cap, width), F32), vmem((tiles, 1, slots), F32),
            vmem((2, slots, width), F32), vmem((2, tiles, 1, slots), F32),
            vmem((2, width), jnp.int32), vmem((2, width), jnp.int32),
            vmem((width, width), F32), vmem((width, width), F32),
            vmem((width, width), F32), vmem((width, width), F32),
            vmem((width, width), BF16), vmem((width, width), BF16),
            vmem((width, width), BF16), vmem((width, width), BF16),
            vmem((width, width), F32), vmem((width, width), F32),
            vmem((step, width), F32), vmem((half, width), F32),
            vmem((8, 128), F32), vmem((count, 8, 128), F32),
            dma((2,)), dma((2, tiles // 2)), dma((2, tiles)), dma((2,)), dma((2,)), dma((tiles,)), dma((tiles,)),
            dma((tiles,)), dma((1,)), dma((1,)), dma((1,)),
            dma((2, bits)), dma((bits,)), dma((bits,)), dma((count,)), dma((count,)),
        ],
        compiler_params=pltpu.CompilerParams(
            collective_id=0, has_side_effects=True, vmem_limit_bytes=40 * 1024 * 1024),
    )(slice_rows, row_owner, leaf_row.reshape(1, rows), exponent.reshape(1, rows),
      environment, ordering, sign_mask)
    spread = jnp.sqrt(square[0, 0] / (width * width) + 1e-06)
    return block / spread, jnp.log(spread).reshape(1)


def from_partner(x, axis, bit):
    return lax.ppermute(x, axis, [(i, i ^ 1 << bit) for i in range(lax.axis_size(axis))])


def multiply(left_factor, right_factor):
    return jnp.dot(
        left_factor,
        right_factor,
        precision=lax.Precision.HIGHEST,
        preferred_element_type=jnp.float32,
    )


def plain_body(slice_rows, row_owner, leaf_row, exponent, environment, ordering, sign_mask):
    tiles = lax.axis_size("tile")
    cut_count = lax.axis_size("cuts")
    width = slice_rows.shape[1]
    row_count = slice_rows.shape[0]
    capacity = max(2, (3 * row_count + 2 * tiles - 1) // (2 * tiles))
    factor = jnp.where(exponent == -1, 0.5, jnp.where(exponent == 1, 2.0, 1.0)).astype(jnp.float32)
    scaled = slice_rows * factor[:, None]
    owners = row_owner[:, 0]
    hits = (owners[:, None] == jnp.arange(tiles, dtype=jnp.int32)[None, :]).astype(jnp.int32)
    before = jnp.cumsum(hits, axis=0) - hits
    position = jnp.sum(before * hits, axis=1)
    placed = owners * capacity + position
    outgoing = jnp.zeros((tiles * capacity, width), jnp.float32).at[placed].set(scaled)
    outgoing_rows = jnp.zeros((tiles * capacity,), jnp.int32).at[placed].set(leaf_row)
    arrived, arrived_rows = (
        lax.all_to_all(outgoing, "tile", split_axis=0, concat_axis=0, tiled=True),
        lax.all_to_all(outgoing_rows, "tile", split_axis=0, concat_axis=0, tiled=True),
    )
    collected = jnp.zeros((width, width), jnp.float32).at[arrived_rows].add(arrived)
    contracted = multiply(collected, environment)
    columns = jnp.arange(width, dtype=jnp.int32)
    signs = 1.0 - 2.0 * sign_mask[0].astype(jnp.float32)
    signed = (ordering[0][:, None] == columns[None, :]).astype(jnp.float32) * signs[:, None]
    product = contracted + signed
    for level in range(tiles.bit_length() - 1):
        partner = from_partner(product, "tile", level)
        upper = lax.axis_index("tile") >> level & 1 == 1
        first_part = jnp.where(upper, partner, product)
        second_part = jnp.where(upper, product, partner)
        product = multiply(first_part, second_part)
    level = 0
    partner = from_partner(product, "cuts", level)
    upper = lax.axis_index("cuts") >> level & 1 == 1
    first_part = jnp.where(upper, partner, product)
    second_part = jnp.where(upper, product, partner)
    product = multiply(first_part, second_part)
    spread = jnp.sqrt(jnp.mean(product * product) + 1e-06)
    rows_each = width // tiles
    cols_each = width // cut_count
    row_start = lax.axis_index("tile") * rows_each
    col_start = lax.axis_index("cuts") * cols_each
    own_block = lax.dynamic_slice(product, (row_start, col_start), (rows_each, cols_each))
    return (own_block / spread, jnp.log(spread).reshape(1))


def solution(mesh):
    tiles, cuts = mesh.shape["tile"], mesh.shape["cuts"]
    fits = cuts == 2 and 4 <= tiles <= 16
    return jax.shard_map(
        body if fits else plain_body,
        mesh=mesh,
        in_specs=(
            P(("groups", "tile", "cuts"), None),
            P(("groups", "tile", "cuts"), None),
            P(("groups", "tile", "cuts")),
            P(("groups", "tile", "cuts")),
            P(("groups", "tile", "cuts"), None),
            P(("groups", "tile", "cuts"), None),
            P(("groups", "tile", "cuts"), None),
        ),
        out_specs=(P(("groups", "tile"), "cuts"), P("groups")),
        check_vma=False,
    )
```

```python
import functools

import jax
import jax.numpy as jnp
from jax import lax
from jax.experimental import pallas as pl
from jax.experimental.pallas import tpu as pltpu
from jax.sharding import PartitionSpec as P

MESH = pl.DeviceIdType.MESH
F32, BF16 = jnp.float32, jnp.bfloat16
NN = (((1,), (0,)), ((), ()))
NT = (((1,), (1,)), ((), ()))


def halves(x):
    high = x.astype(BF16)
    return high, (x - high.astype(F32)).astype(BF16)


def dot(a, b, dims=NN):
    return lax.dot_general(a, b, dims, preferred_element_type=F32)


def dot3(left, right, dims=NN):
    return (dot(left[0], right[1], dims) + dot(left[1], right[0], dims)) + dot(left[0], right[0], dims)


def kernel(tiles, cap, parts,
           rows_ref, owner_ref, leaf_row_ref, exponent_ref, env_ref, ordering_ref, sign_ref,
           block_ref, square_ref,
           rows_in, env_in, out_rows, out_ids, in_rows, in_ids, bond_out, bond_in, env_out, env_far,
           own, far, own_high, own_low, chain_high, chain_low,
           turned_high, turned_low, seated,
           chain_in, chain_out, p_in, q_in, sums_out, sums_in,
           load, route_send, route_recv, far_send, far_recv, chain_send, chain_recv,
           p_send, p_recv, pass_send, pass_recv, q_send, q_recv, half_send, sum_send, sum_recv):
    group, me, cut = lax.axis_index("groups"), lax.axis_index("tile"), lax.axis_index("cuts")
    load_env = pltpu.make_async_copy(env_ref, env_in, load.at[0])
    load_rows = pltpu.make_async_copy(rows_ref, rows_in, load.at[1])
    load_env.start()
    load_rows.start()
    rows, width = rows_ref.shape
    step = width // tiles
    pairs = tiles // 2
    bits = pairs * parts
    bit_rows = step // parts
    slots = tiles * cap
    lane = 128 // 2
    count = 2 * tiles
    ident = me * 2 + cut
    place = jnp.where(cut == 0, me, tiles - 1 - me)
    way = 1 - 2 * cut
    last = place == tiles - 1
    host = lax.rem(place, 2) == 1
    pair_me = me // 2

    def chunk(ref, k):
        return ref.at[pl.ds(pl.multiple_of(k * step, 8), step)]

    def part(ref, i):
        return ref.at[pl.ds(pl.multiple_of(i * bit_rows, 8), bit_rows)]

    def remote(src, dst, send, recv, tile, other):
        return pltpu.make_async_remote_copy(
            src_ref=src, dst_ref=dst, send_sem=send, recv_sem=recv,
            device_id=(group, tile, other), device_id_type=MESH)

    barrier = pltpu.get_barrier_semaphore()

    @pl.loop(1, count)
    def _(d):
        peer = lax.rem(ident + d, count)
        pl.semaphore_signal(barrier, inc=1, device_id=(group, peer // 2, lax.rem(peer, 2)), device_id_type=MESH)

    bond_out[0:1] = ordering_ref[...]
    bond_out[1:2] = sign_ref[...]
    load_env.wait()

    @pl.when(cut == 0)
    def _():
        env_out[...] = env_in[...]

    @pl.when(cut == 1)
    def _():
        env_out[...] = env_in[...].T

    def to_host():
        to = lax.rem(me + way + tiles, tiles)
        return (remote(bond_out, bond_in, far_send.at[0], far_recv.at[0], to, cut),
                remote(env_out, env_far, far_send.at[1], far_recv.at[1], to, cut))

    pl.semaphore_wait(barrier, count - 1)

    @pl.when(jnp.logical_not(host))
    def _():
        for copy in to_host():
            copy.start()

    load_rows.wait()
    level = exponent_ref[...]
    factor = jnp.where(level == -1, 0.5, jnp.where(level == 1, 2.0, 1.0)).astype(F32)
    factor = jnp.broadcast_to(factor, (128, rows)).T[:, 0:1]
    scaled = rows_in[...] * factor
    owner = owner_ref[...]
    hits = (owner == lax.broadcasted_iota(jnp.int32, (rows, 128), 1)).astype(F32)
    earlier = (lax.broadcasted_iota(jnp.int32, (rows, rows), 1)
               < lax.broadcasted_iota(jnp.int32, (rows, rows), 0)).astype(F32)
    before = dot(earlier.astype(BF16), hits.astype(BF16))
    position = jnp.sum(before * hits, axis=1, keepdims=True)
    position = jnp.broadcast_to(position, (rows, 128)).T[0:1, :].astype(jnp.int32)
    owner = jnp.broadcast_to(owner.astype(F32), (rows, 128)).T[0:1, :].astype(jnp.int32)
    slot = lax.broadcasted_iota(jnp.int32, (slots, rows), 0)
    pick = (slot == owner * cap + position).astype(F32).astype(BF16)
    high = scaled.astype(BF16)
    rest = scaled - high.astype(F32)
    middle = rest.astype(BF16)
    low = (rest - middle.astype(F32)).astype(BF16)
    out_rows[...] = ((dot(pick, low) + dot(pick, middle)) + dot(pick, high)).reshape(tiles, cap, width)
    seat = (lax.broadcasted_iota(jnp.int32, (128, rows), 0) == lax.rem(me, 2) * lane + position)
    seat = seat.astype(F32).astype(BF16)
    named = jnp.where(lax.broadcasted_iota(jnp.int32, (tiles, rows), 0) == owner,
                      leaf_row_ref[...] + 1, 0).astype(F32)
    named_high, named_low = halves(named)
    ids = dot(named_high, seat, NT) + dot(named_low, seat, NT)
    for t in range(tiles):
        out_ids[t] = ids[t:t + 1, :]

    def slots_of(source):
        return pl.ds(pl.multiple_of(source * lane, 8), cap)

    def route(pair, source):
        both = pl.ds(2 * pair, 2)
        to = 2 * pair + 1 - cut
        return (remote(out_rows.at[both], in_rows.at[:, slots_of(source)], route_send.at[0, pair],
                       route_recv.at[0, source], to, cut),
                remote(out_ids.at[both], in_ids.at[:, source], route_send.at[1, pair],
                       route_recv.at[1, source], to, cut))

    @pl.loop(1, pairs)
    def _(d):
        for copy in route(lax.rem(pair_me + d, pairs), me):
            copy.start()

    @pl.when(jnp.logical_not(host))
    def _():
        for copy in route(pair_me, me):
            copy.start()

    def bond_of(order, sign):
        return jnp.where(lax.broadcasted_iota(jnp.int32, (width, width), 0) == order,
                         (1 - 2 * sign).astype(F32), 0.0)

    @pl.when(host)
    def _():
        for c in range(2):
            in_rows[c, slots_of(me)] = out_rows[2 * pair_me + c]
            in_ids[c, me] = out_ids[2 * pair_me + c]
        to_host()[0].wait_recv()

        @pl.when(cut == 0)
        def _():
            own[...] = bond_of(bond_out[0:1], bond_out[1:2]).T
            far[...] = bond_of(bond_in[0:1], bond_in[1:2]).T

        @pl.when(cut == 1)
        def _():
            own[...] = bond_of(bond_out[0:1], bond_out[1:2])
            far[...] = bond_of(bond_in[0:1], bond_in[1:2])

        for t in range(tiles):
            if cap < lane:
                in_rows[:, t * lane + cap:(t + 1) * lane] = jnp.zeros((2, lane - cap, width), F32)
        own_high[...], own_low[...] = halves(env_out[...])
        to_host()[1].wait_recv()
        chain_high[...], chain_low[...] = halves(env_far[...])

        @pl.loop(0, pairs)
        def _(d):
            pair = lax.rem(jnp.where(pair_me < pairs // 2, pair_me + d, pair_me + pairs - d), pairs)
            for c in range(2):
                @pl.when(2 * pair + c != me)
                def _():
                    for copy in route(pair_me, 2 * pair + c):
                        copy.wait_recv()
            lanes = pl.ds(pl.multiple_of(pair * 128, 128), 128)

            for c in range(2):
                wanted = (in_ids[c, 2 * pair] + in_ids[c, 2 * pair + 1]).astype(jnp.int32) - 1
                seated[c, :, lanes] = (
                    lax.broadcasted_iota(jnp.int32, (width, 128), 0) == wanted).astype(F32).astype(BF16)

            def turn(c, environment):
                arrived = halves(in_rows[c, lanes])

                @pl.when(cut == 0)
                def _():
                    turned_high[c, lanes], turned_low[c, lanes] = halves(dot3(arrived, environment))

                @pl.when(cut == 1)
                def _():
                    turned_high[c, :, lanes], turned_low[c, :, lanes] = halves(dot3(environment, arrived, NT))

            turn(1 - cut, (own_high[...], own_low[...]))
            turn(cut, (chain_high[...], chain_low[...]))

        @pl.when(cut == 0)
        def _():
            own[...] += dot(seated[1], turned_low[1]) + dot(seated[1], turned_high[1])
            far[...] += dot(seated[0], turned_low[0]) + dot(seated[0], turned_high[0])

        @pl.when(cut == 1)
        def _():
            own[...] += dot(turned_low[0], seated[0], NT) + dot(turned_high[0], seated[0], NT)
            far[...] += dot(turned_low[1], seated[1], NT) + dot(turned_high[1], seated[1], NT)

        own_high[...], own_low[...] = halves(own[...])

    def link(k):
        return remote(chunk(chain_out, k), chunk(chain_in, k), chain_send.at[k], chain_recv.at[k],
                      lax.rem(me + 2 * way + tiles, tiles), cut)

    def p_copy(k):
        return remote(chunk(chain_out, k), p_in, p_send.at[k], p_recv.at[0], k, 0)

    def q_along(i):
        return remote(part(q_in, i), part(q_in, i), q_send.at[0, i], q_recv.at[i], lax.rem(me + 2, tiles), cut)

    def q_across(i):
        return remote(part(q_in, i), part(q_in, i), q_send.at[1, i], q_recv.at[i], lax.rem(me + 1, tiles), cut)

    def q_half(i):
        return remote(part(chain_out, i), part(q_in, i), half_send.at[i], q_recv.at[i], 0, 0)

    even_tile = lax.rem(me, 2) == 0
    p_root = jnp.logical_and(last, cut == 0)
    q_root = jnp.logical_and(last, cut == 1)

    def emit(k, value):
        at = pl.ds(pl.multiple_of(k * step, 8), step)

        @pl.when(jnp.logical_not(last))
        def _():
            chain_out[at] = value
            link(k).start()

        @pl.when(p_root)
        def _():
            @pl.when(k < tiles - 1)
            def _():
                chain_out[at] = value
                p_copy(k).start()

            @pl.when(k == tiles - 1)
            def _():
                p_in[...] = value

        @pl.when(q_root)
        def _():
            @pl.when(k < pairs)
            def _():
                chain_out[at] = value
                for i in range(parts):
                    q_half(k * parts + i).start()

            @pl.when(k >= pairs)
            def _():
                q_in[pl.ds(pl.multiple_of((k - pairs) * step, 8), step)] = value
                for i in range(parts):
                    q_along((k - pairs) * parts + i).start()
                    q_across((k - pairs) * parts + i).start()

    @pl.when(place == 1)
    def _():
        @pl.loop(0, tiles)
        def _(k):
            at = pl.ds(pl.multiple_of(k * step, 8), step)
            emit(k, dot3(halves(far[at]), (own_high[...], own_low[...])))

    @pl.when(jnp.logical_and(host, place > 1))
    def _():
        chain_high[...], chain_low[...] = halves(dot3(halves(far[...]), (own_high[...], own_low[...])))

        @pl.loop(0, tiles)
        def _(k):
            at = pl.ds(pl.multiple_of(k * step, 8), step)
            link(k).wait_recv()
            emit(k, dot3(halves(chain_in[at]), (chain_high[...], chain_low[...])))

    @pl.when(jnp.logical_not(q_root))
    def _():
        @pl.loop(0, bits)
        def _(k):
            q_half(k).wait_recv()

            @pl.when(even_tile)
            def _():
                @pl.when(me < tiles - 2)
                def _():
                    q_along(k).start()

                q_across(k).start()

    def p_pass():
        return remote(p_in, p_in, pass_send.at[0], pass_recv.at[0], me, 1)

    @pl.when(cut == 0)
    def _():
        @pl.when(jnp.logical_not(p_root))
        def _():
            p_copy(0).wait_recv()

        p_pass().start()

    @pl.when(cut == 1)
    def _():
        p_pass().wait_recv()

    result = dot3(halves(p_in[...]), halves(q_in[...]), NT)
    block_ref[...] = result
    total = jnp.sum(jnp.sum(result * result, axis=0, keepdims=True), axis=1, keepdims=True)
    total = jnp.broadcast_to(total, (8, 128))
    sums_out[...] = total

    def share(peer, slot):
        return remote(sums_out, sums_in.at[slot], sum_send.at[peer], sum_recv.at[slot],
                      peer // 2, lax.rem(peer, 2))

    @pl.loop(1, count)
    def _(d):
        share(lax.rem(ident + d, count), ident).start()

    sums_in[ident] = total

    @pl.loop(1, pairs)
    def _(d):
        for copy in route(lax.rem(pair_me + d, pairs), me):
            copy.wait_send()

    @pl.when(jnp.logical_not(host))
    def _():
        for copy in route(pair_me, me) + to_host():
            copy.wait_send()

    @pl.when(jnp.logical_and(host, jnp.logical_not(last)))
    def _():
        @pl.loop(0, tiles)
        def _(k):
            link(k).wait_send()

    @pl.when(p_root)
    def _():
        @pl.loop(0, tiles - 1)
        def _(k):
            p_copy(k).wait_send()

    @pl.when(q_root)
    def _():
        @pl.loop(0, bits)
        def _(k):
            q_half(k).wait_send()

    @pl.when(even_tile)
    def _():
        @pl.loop(0, bits)
        def _(k):
            @pl.when(me < tiles - 2)
            def _():
                q_along(k).wait_send()

            q_across(k).wait_send()

    @pl.when(cut == 0)
    def _():
        p_pass().wait_send()

    @pl.loop(1, count)
    def _(d):
        peer = lax.rem(ident + d, count)
        share(peer, peer).wait_recv()
        share(peer, peer).wait_send()

    square_ref[...] = jnp.sum(sums_in[...], axis=0)


def body(slice_rows, row_owner, leaf_row, exponent, environment, ordering, sign_mask):
    tiles = lax.axis_size("tile")
    rows, width = slice_rows.shape
    step = width // tiles
    half = width // 2
    cap = max(2, (3 * rows + 2 * tiles - 1) // (2 * tiles))
    cap = (cap + 15) // 16 * 16
    if lax.axis_size("cuts") != 2 or cap > 64 or width != tiles * 64:
        return plain_body(slice_rows, row_owner, leaf_row, exponent, environment, ordering, sign_mask)
    places = tiles * 64
    count = 2 * tiles
    parts = 2 if step % 32 == 0 else 1
    bits = tiles // 2 * parts
    vmem, dma = pltpu.VMEM, pltpu.SemaphoreType.DMA
    block, square = pl.pallas_call(
        functools.partial(kernel, tiles, cap, parts),
        out_shape=(jax.ShapeDtypeStruct((step, half), F32), jax.ShapeDtypeStruct((8, 128), F32)),
        in_specs=[pl.BlockSpec(memory_space=pltpu.HBM if i in (0, 4) else vmem) for i in range(7)],
        out_specs=(pl.BlockSpec(memory_space=vmem), pl.BlockSpec(memory_space=vmem)),
        scratch_shapes=[
            vmem((rows, width), F32), vmem((width, width), F32),
            vmem((tiles, cap, width), F32), vmem((tiles, 1, 128), F32),
            vmem((2, places, width), F32), vmem((2, tiles, 1, 128), F32),
            vmem((2, width), jnp.int32), vmem((2, width), jnp.int32),
            vmem((width, width), F32), vmem((width, width), F32),
            vmem((width, width), F32), vmem((width, width), F32),
            vmem((width, width), BF16), vmem((width, width), BF16),
            vmem((width, width), BF16), vmem((width, width), BF16),
            vmem((2, max(width, places), max(width, places)), BF16),
            vmem((2, max(width, places), max(width, places)), BF16), vmem((2, width, places), BF16),
            vmem((width, width), F32), vmem((width, width), F32),
            vmem((step, width), F32), vmem((half, width), F32),
            vmem((8, 128), F32), vmem((count, 8, 128), F32),
            dma((2,)), dma((2, tiles // 2)), dma((2, tiles)), dma((2,)), dma((2,)), dma((tiles,)), dma((tiles,)),
            dma((tiles,)), dma((1,)), dma((1,)), dma((1,)),
            dma((2, bits)), dma((bits,)), dma((bits,)), dma((count,)), dma((count,)),
        ],
        compiler_params=pltpu.CompilerParams(
            collective_id=0, has_side_effects=True, vmem_limit_bytes=40 * 1024 * 1024),
    )(slice_rows, row_owner, leaf_row.reshape(1, rows), exponent.reshape(1, rows),
      environment, ordering, sign_mask)
    spread = jnp.sqrt(square[0, 0] / (width * width) + 1e-06)
    return block / spread, jnp.log(spread).reshape(1)


def from_partner(x, axis, bit):
    return lax.ppermute(x, axis, [(i, i ^ 1 << bit) for i in range(lax.axis_size(axis))])


def multiply(left_factor, right_factor):
    return jnp.dot(
        left_factor,
        right_factor,
        precision=lax.Precision.HIGHEST,
        preferred_element_type=jnp.float32,
    )


def plain_body(slice_rows, row_owner, leaf_row, exponent, environment, ordering, sign_mask):
    tiles = lax.axis_size("tile")
    cut_count = lax.axis_size("cuts")
    width = slice_rows.shape[1]
    row_count = slice_rows.shape[0]
    capacity = max(2, (3 * row_count + 2 * tiles - 1) // (2 * tiles))
    factor = jnp.where(exponent == -1, 0.5, jnp.where(exponent == 1, 2.0, 1.0)).astype(jnp.float32)
    scaled = slice_rows * factor[:, None]
    owners = row_owner[:, 0]
    hits = (owners[:, None] == jnp.arange(tiles, dtype=jnp.int32)[None, :]).astype(jnp.int32)
    before = jnp.cumsum(hits, axis=0) - hits
    position = jnp.sum(before * hits, axis=1)
    placed = owners * capacity + position
    outgoing = jnp.zeros((tiles * capacity, width), jnp.float32).at[placed].set(scaled)
    outgoing_rows = jnp.zeros((tiles * capacity,), jnp.int32).at[placed].set(leaf_row)
    arrived, arrived_rows = (
        lax.all_to_all(outgoing, "tile", split_axis=0, concat_axis=0, tiled=True),
        lax.all_to_all(outgoing_rows, "tile", split_axis=0, concat_axis=0, tiled=True),
    )
    collected = jnp.zeros((width, width), jnp.float32).at[arrived_rows].add(arrived)
    contracted = multiply(collected, environment)
    columns = jnp.arange(width, dtype=jnp.int32)
    signs = 1.0 - 2.0 * sign_mask[0].astype(jnp.float32)
    signed = (ordering[0][:, None] == columns[None, :]).astype(jnp.float32) * signs[:, None]
    product = contracted + signed
    for level in range(tiles.bit_length() - 1):
        partner = from_partner(product, "tile", level)
        upper = lax.axis_index("tile") >> level & 1 == 1
        first_part = jnp.where(upper, partner, product)
        second_part = jnp.where(upper, product, partner)
        product = multiply(first_part, second_part)
    level = 0
    partner = from_partner(product, "cuts", level)
    upper = lax.axis_index("cuts") >> level & 1 == 1
    first_part = jnp.where(upper, partner, product)
    second_part = jnp.where(upper, product, partner)
    product = multiply(first_part, second_part)
    spread = jnp.sqrt(jnp.mean(product * product) + 1e-06)
    rows_each = width // tiles
    cols_each = width // cut_count
    row_start = lax.axis_index("tile") * rows_each
    col_start = lax.axis_index("cuts") * cols_each
    own_block = lax.dynamic_slice(product, (row_start, col_start), (rows_each, cols_each))
    return (own_block / spread, jnp.log(spread).reshape(1))


def solution(mesh):
    return jax.shard_map(
        body,
        mesh=mesh,
        in_specs=(
            P(("groups", "tile", "cuts"), None),
            P(("groups", "tile", "cuts"), None),
            P(("groups", "tile", "cuts")),
            P(("groups", "tile", "cuts")),
            P(("groups", "tile", "cuts"), None),
            P(("groups", "tile", "cuts"), None),
            P(("groups", "tile", "cuts"), None),
        ),
        out_specs=(P(("groups", "tile"), "cuts"), P("groups")),
        check_vma=False,
    )
```

```python
import functools

import jax
import jax.numpy as jnp
from jax import lax
from jax.experimental import pallas as pl
from jax.experimental.pallas import tpu as pltpu
from jax.sharding import PartitionSpec as P

MESH = pl.DeviceIdType.MESH
F32, BF16 = jnp.float32, jnp.bfloat16
NN = (((1,), (0,)), ((), ()))
NT = (((1,), (1,)), ((), ()))


def halves(x):
    high = x.astype(BF16)
    return high, (x - high.astype(F32)).astype(BF16)


def dot(a, b, dims=NN):
    return lax.dot_general(a, b, dims, preferred_element_type=F32)


def dot3(left, right, dims=NN):
    return (dot(left[0], right[1], dims) + dot(left[1], right[0], dims)) + dot(left[0], right[0], dims)


def kernel(tiles, cap, parts,
           rows_ref, owner_ref, leaf_row_ref, exponent_ref, env_ref, ordering_ref, sign_ref,
           block_ref, square_ref,
           rows_in, env_in, out_rows, out_ids, in_rows, in_ids, bond_out, bond_in, turn_out, turn_in,
           own, far, own_high, own_low, chain_high, chain_low,
           turned_high, turned_low, seated,
           chain_in, chain_out, p_in, q_in, sums_out, sums_in,
           load, route_send, route_recv, ids_send, ids_recv, bond_send, bond_recv, turn_send, turn_recv, chain_send, chain_recv,
           p_send, p_recv, pass_send, pass_recv, q_send, q_recv, half_send, sum_send, sum_recv):
    group, me, cut = lax.axis_index("groups"), lax.axis_index("tile"), lax.axis_index("cuts")
    load_env = pltpu.make_async_copy(env_ref, env_in, load.at[0])
    load_rows = pltpu.make_async_copy(rows_ref, rows_in, load.at[1])
    load_env.start()
    load_rows.start()
    rows, width = rows_ref.shape
    step = width // tiles
    pairs = tiles // 2
    bits = pairs * parts
    bit_rows = step // parts
    slots = tiles * cap
    lane = 128 // 2
    count = 2 * tiles
    ident = me * 2 + cut
    place = jnp.where(cut == 0, me, tiles - 1 - me)
    way = 1 - 2 * cut
    last = place == tiles - 1
    host = lax.rem(place, 2) == 1
    pair_me = me // 2

    def chunk(ref, k):
        return ref.at[pl.ds(pl.multiple_of(k * step, 8), step)]

    def part(ref, i):
        return ref.at[pl.ds(pl.multiple_of(i * bit_rows, 8), bit_rows)]

    def remote(src, dst, send, recv, tile, other):
        return pltpu.make_async_remote_copy(
            src_ref=src, dst_ref=dst, send_sem=send, recv_sem=recv,
            device_id=(group, tile, other), device_id_type=MESH)

    barrier = pltpu.get_barrier_semaphore()

    @pl.loop(1, count)
    def _(d):
        peer = lax.rem(ident + d, count)
        pl.semaphore_signal(barrier, inc=1, device_id=(group, peer // 2, lax.rem(peer, 2)), device_id_type=MESH)

    bond_out[0:1] = ordering_ref[...]
    bond_out[1:2] = sign_ref[...]
    load_env.wait()
    own_high[...], own_low[...] = halves(env_in[...])

    def bond_copy():
        return remote(bond_out, bond_in, bond_send.at[0], bond_recv.at[0], lax.rem(me + way + tiles, tiles), cut)

    pl.semaphore_wait(barrier, count - 1)

    @pl.when(jnp.logical_not(host))
    def _():
        bond_copy().start()

    load_rows.wait()
    level = exponent_ref[...]
    factor = jnp.where(level == -1, 0.5, jnp.where(level == 1, 2.0, 1.0)).astype(F32)
    factor = jnp.broadcast_to(factor, (128, rows)).T[:, 0:1]
    scaled = rows_in[...] * factor
    owner = owner_ref[...]
    hits = (owner == lax.broadcasted_iota(jnp.int32, (rows, 128), 1)).astype(F32)
    earlier = (lax.broadcasted_iota(jnp.int32, (rows, rows), 1)
               < lax.broadcasted_iota(jnp.int32, (rows, rows), 0)).astype(F32)
    before = dot(earlier.astype(BF16), hits.astype(BF16))
    position = jnp.sum(before * hits, axis=1, keepdims=True)
    position = jnp.broadcast_to(position, (rows, 128)).T[0:1, :].astype(jnp.int32)
    owner = jnp.broadcast_to(owner.astype(F32), (rows, 128)).T[0:1, :].astype(jnp.int32)
    slot = lax.broadcasted_iota(jnp.int32, (slots, rows), 0)
    pick = (slot == owner * cap + position).astype(F32).astype(BF16)
    high = scaled.astype(BF16)
    rest = scaled - high.astype(F32)
    middle = rest.astype(BF16)
    low = (rest - middle.astype(F32)).astype(BF16)
    out_rows[...] = (dot(pick, low) + dot(pick, middle)) + dot(pick, high)
    seat = (lax.broadcasted_iota(jnp.int32, (128, rows), 0) == lax.rem(me, 2) * lane + position)
    seat = seat.astype(F32).astype(BF16)
    named = jnp.where(lax.broadcasted_iota(jnp.int32, (tiles, rows), 0) == owner,
                      leaf_row_ref[...] + 1, 0).astype(F32)
    named_high, named_low = halves(named)
    ids = dot(named_high, seat, NT) + dot(named_low, seat, NT)
    for t in range(tiles):
        out_ids[t] = ids[t:t + 1, :]

    def slots_of(source):
        return pl.ds(pl.multiple_of(source * lane, 8), cap)

    def route(to, source):
        return remote(out_rows.at[pl.ds(pl.multiple_of(to * cap, 8), cap)], in_rows.at[slots_of(source)],
                      route_send.at[to], route_recv.at[source], to, cut)

    def route_ids(pair, source):
        return remote(out_ids.at[pl.ds(2 * pair, 2)], in_ids.at[:, source],
                      ids_send.at[pair], ids_recv.at[source], 2 * pair + 1 - cut, cut)

    @pl.loop(1, tiles)
    def _(d):
        route(lax.rem(me + d, tiles), me).start()

    @pl.loop(1, pairs)
    def _(d):
        route_ids(lax.rem(pair_me + d, pairs), me).start()

    @pl.when(jnp.logical_not(host))
    def _():
        route_ids(pair_me, me).start()

    def bond_of(order, sign):
        return jnp.where(lax.broadcasted_iota(jnp.int32, (width, width), 0) == order,
                         (1 - 2 * sign).astype(F32), 0.0)

    in_rows[slots_of(me)] = out_rows[pl.ds(pl.multiple_of(me * cap, 8), cap)]
    for t in range(tiles):
        if cap < lane:
            in_rows[t * lane + cap:(t + 1) * lane] = jnp.zeros((lane - cap, width), F32)

    def pair_at(d):
        return lax.rem(jnp.where(pair_me < pairs // 2, pair_me + d, pair_me + pairs - d), pairs)

    def lanes_of(pair):
        return pl.ds(pl.multiple_of(pair * 128, 128), 128)

    def turn(pair):
        for c in range(2):
            @pl.when(2 * pair + c != me)
            def _():
                route(2 * pair + c, 2 * pair + c).wait_recv()
        return dot3(halves(in_rows[lanes_of(pair)]), (own_high[...], own_low[...]))

    def turn_copy(pair):
        return remote(turn_out.at[lanes_of(pair)], turn_in.at[lanes_of(pair)],
                      turn_send.at[pair], turn_recv.at[pair], lax.rem(me + way + tiles, tiles), cut)

    @pl.when(jnp.logical_not(host))
    def _():
        @pl.loop(0, pairs)
        def _(d):
            pair = pair_at(d)
            turn_out[lanes_of(pair)] = turn(pair)
            turn_copy(pair).start()

    @pl.when(host)
    def _():
        for c in range(2):
            in_ids[c, me] = out_ids[2 * pair_me + c]
        bond_copy().wait_recv()

        @pl.when(cut == 0)
        def _():
            own[...] = bond_of(bond_out[0:1], bond_out[1:2]).T
            far[...] = bond_of(bond_in[0:1], bond_in[1:2]).T

        @pl.when(cut == 1)
        def _():
            own[...] = bond_of(bond_out[0:1], bond_out[1:2])
            far[...] = bond_of(bond_in[0:1], bond_in[1:2])

        def keep(c, pair, value):
            lanes = lanes_of(pair)

            @pl.when(cut == 0)
            def _():
                turned_high[c, lanes], turned_low[c, lanes] = halves(value)

            @pl.when(cut == 1)
            def _():
                turned_high[c, :, lanes], turned_low[c, :, lanes] = halves(value.T)

        def keep_far(pair):
            turn_copy(pair).wait_recv()
            keep(0, pair, turn_in[lanes_of(pair)])

        @pl.loop(0, pairs)
        def _(d):
            pair = pair_at(d)
            keep(1, pair, turn(pair))
            for c in range(2):
                @pl.when(2 * pair + c != me)
                def _():
                    route_ids(pair_me, 2 * pair + c).wait_recv()
            for c in range(2):
                named_there = jnp.where(cut == 0, c, 1 - c)
                wanted = (in_ids[named_there, 2 * pair] + in_ids[named_there, 2 * pair + 1]).astype(jnp.int32) - 1
                seated[c, :, lanes_of(pair)] = (
                    lax.broadcasted_iota(jnp.int32, (width, 128), 0) == wanted).astype(F32).astype(BF16)

            @pl.when(d > 0)
            def _():
                keep_far(pair_at(d - 1))

        def leaf(ref, c):
            @pl.when(cut == 0)
            def _():
                ref[...] += dot(seated[c], turned_low[c]) + dot(seated[c], turned_high[c])

            @pl.when(cut == 1)
            def _():
                ref[...] += dot(turned_low[c], seated[c], NT) + dot(turned_high[c], seated[c], NT)

        leaf(own, 1)
        own_high[...], own_low[...] = halves(own[...])
        keep_far(pair_at(pairs - 1))
        leaf(far, 0)

    def link(k):
        return remote(chunk(chain_out, k), chunk(chain_in, k), chain_send.at[k], chain_recv.at[k],
                      lax.rem(me + 2 * way + tiles, tiles), cut)

    def p_copy(k):
        return remote(chunk(chain_out, k), p_in, p_send.at[k], p_recv.at[0], k, 0)

    def q_along(i):
        return remote(part(q_in, i), part(q_in, i), q_send.at[0, i], q_recv.at[i], lax.rem(me + 2, tiles), cut)

    def q_across(i):
        return remote(part(q_in, i), part(q_in, i), q_send.at[1, i], q_recv.at[i], lax.rem(me + 1, tiles), cut)

    def q_half(i):
        return remote(part(chain_out, i), part(q_in, i), half_send.at[i], q_recv.at[i], 0, 0)

    even_tile = lax.rem(me, 2) == 0
    p_root = jnp.logical_and(last, cut == 0)
    q_root = jnp.logical_and(last, cut == 1)

    def emit(k, value):
        at = pl.ds(pl.multiple_of(k * step, 8), step)

        @pl.when(jnp.logical_not(last))
        def _():
            chain_out[at] = value
            link(k).start()

        @pl.when(p_root)
        def _():
            @pl.when(k < tiles - 1)
            def _():
                chain_out[at] = value
                p_copy(k).start()

            @pl.when(k == tiles - 1)
            def _():
                p_in[...] = value

        @pl.when(q_root)
        def _():
            @pl.when(k < pairs)
            def _():
                chain_out[at] = value
                for i in range(parts):
                    q_half(k * parts + i).start()

            @pl.when(k >= pairs)
            def _():
                q_in[pl.ds(pl.multiple_of((k - pairs) * step, 8), step)] = value
                for i in range(parts):
                    q_along((k - pairs) * parts + i).start()
                    q_across((k - pairs) * parts + i).start()

    @pl.when(place == 1)
    def _():
        @pl.loop(0, tiles)
        def _(k):
            at = pl.ds(pl.multiple_of(k * step, 8), step)
            emit(k, dot3(halves(far[at]), (own_high[...], own_low[...])))

    @pl.when(jnp.logical_and(host, place > 1))
    def _():
        chain_high[...], chain_low[...] = halves(dot3(halves(far[...]), (own_high[...], own_low[...])))

        @pl.loop(0, tiles)
        def _(k):
            at = pl.ds(pl.multiple_of(k * step, 8), step)
            link(k).wait_recv()
            emit(k, dot3(halves(chain_in[at]), (chain_high[...], chain_low[...])))

    @pl.when(jnp.logical_not(q_root))
    def _():
        @pl.loop(0, bits)
        def _(k):
            q_half(k).wait_recv()

            @pl.when(even_tile)
            def _():
                @pl.when(me < tiles - 2)
                def _():
                    q_along(k).start()

                q_across(k).start()

    def p_pass():
        return remote(p_in, p_in, pass_send.at[0], pass_recv.at[0], me, 1)

    @pl.when(cut == 0)
    def _():
        @pl.when(jnp.logical_not(p_root))
        def _():
            p_copy(0).wait_recv()

        p_pass().start()

    @pl.when(cut == 1)
    def _():
        p_pass().wait_recv()

    result = dot3(halves(p_in[...]), halves(q_in[...]), NT)
    block_ref[...] = result
    total = jnp.sum(jnp.sum(result * result, axis=0, keepdims=True), axis=1, keepdims=True)
    total = jnp.broadcast_to(total, (8, 128))
    sums_out[...] = total

    def share(peer, slot):
        return remote(sums_out, sums_in.at[slot], sum_send.at[peer], sum_recv.at[slot],
                      peer // 2, lax.rem(peer, 2))

    @pl.loop(1, count)
    def _(d):
        share(lax.rem(ident + d, count), ident).start()

    sums_in[ident] = total

    @pl.loop(1, tiles)
    def _(d):
        route(lax.rem(me + d, tiles), me).wait_send()

    @pl.loop(1, pairs)
    def _(d):
        route_ids(lax.rem(pair_me + d, pairs), me).wait_send()

    @pl.when(jnp.logical_not(host))
    def _():
        route_ids(pair_me, me).wait_send()
        bond_copy().wait_send()

        @pl.loop(0, pairs)
        def _(pair):
            turn_copy(pair).wait_send()

    @pl.when(jnp.logical_and(host, jnp.logical_not(last)))
    def _():
        @pl.loop(0, tiles)
        def _(k):
            link(k).wait_send()

    @pl.when(p_root)
    def _():
        @pl.loop(0, tiles - 1)
        def _(k):
            p_copy(k).wait_send()

    @pl.when(q_root)
    def _():
        @pl.loop(0, bits)
        def _(k):
            q_half(k).wait_send()

    @pl.when(even_tile)
    def _():
        @pl.loop(0, bits)
        def _(k):
            @pl.when(me < tiles - 2)
            def _():
                q_along(k).wait_send()

            q_across(k).wait_send()

    @pl.when(cut == 0)
    def _():
        p_pass().wait_send()

    @pl.loop(1, count)
    def _(d):
        peer = lax.rem(ident + d, count)
        share(peer, peer).wait_recv()
        share(peer, peer).wait_send()

    square_ref[...] = jnp.sum(sums_in[...], axis=0)


def body(slice_rows, row_owner, leaf_row, exponent, environment, ordering, sign_mask):
    tiles = lax.axis_size("tile")
    rows, width = slice_rows.shape
    step = width // tiles
    half = width // 2
    cap = max(2, (3 * rows + 2 * tiles - 1) // (2 * tiles))
    cap = (cap + 15) // 16 * 16
    if lax.axis_size("cuts") != 2 or cap > 64 or width != tiles * 64:
        return plain_body(slice_rows, row_owner, leaf_row, exponent, environment, ordering, sign_mask)
    places = tiles * 64
    count = 2 * tiles
    parts = 2 if step % 32 == 0 else 1
    bits = tiles // 2 * parts
    vmem, dma = pltpu.VMEM, pltpu.SemaphoreType.DMA
    block, square = pl.pallas_call(
        functools.partial(kernel, tiles, cap, parts),
        out_shape=(jax.ShapeDtypeStruct((step, half), F32), jax.ShapeDtypeStruct((8, 128), F32)),
        in_specs=[pl.BlockSpec(memory_space=pltpu.HBM if i in (0, 4) else vmem) for i in range(7)],
        out_specs=(pl.BlockSpec(memory_space=vmem), pl.BlockSpec(memory_space=vmem)),
        scratch_shapes=[
            vmem((rows, width), F32), vmem((width, width), F32),
            vmem((tiles * cap, width), F32), vmem((tiles, 1, 128), F32),
            vmem((places, width), F32), vmem((2, tiles, 1, 128), F32),
            vmem((2, width), jnp.int32), vmem((2, width), jnp.int32),
            vmem((places, width), F32), vmem((places, width), F32),
            vmem((width, width), F32), vmem((width, width), F32),
            vmem((width, width), BF16), vmem((width, width), BF16),
            vmem((width, width), BF16), vmem((width, width), BF16),
            vmem((2, max(width, places), max(width, places)), BF16),
            vmem((2, max(width, places), max(width, places)), BF16), vmem((2, width, places), BF16),
            vmem((width, width), F32), vmem((width, width), F32),
            vmem((step, width), F32), vmem((half, width), F32),
            vmem((8, 128), F32), vmem((count, 8, 128), F32),
            dma((2,)), dma((tiles,)), dma((tiles,)), dma((tiles // 2,)), dma((tiles,)), dma((1,)), dma((1,)),
            dma((tiles // 2,)), dma((tiles // 2,)), dma((tiles,)), dma((tiles,)),
            dma((tiles,)), dma((1,)), dma((1,)), dma((1,)),
            dma((2, bits)), dma((bits,)), dma((bits,)), dma((count,)), dma((count,)),
        ],
        compiler_params=pltpu.CompilerParams(
            collective_id=0, has_side_effects=True, vmem_limit_bytes=60 * 1024 * 1024),
    )(slice_rows, row_owner, leaf_row.reshape(1, rows), exponent.reshape(1, rows),
      environment, ordering, sign_mask)
    spread = jnp.sqrt(square[0, 0] / (width * width) + 1e-06)
    return block / spread, jnp.log(spread).reshape(1)


def from_partner(x, axis, bit):
    return lax.ppermute(x, axis, [(i, i ^ 1 << bit) for i in range(lax.axis_size(axis))])


def multiply(left_factor, right_factor):
    return jnp.dot(
        left_factor,
        right_factor,
        precision=lax.Precision.HIGHEST,
        preferred_element_type=jnp.float32,
    )


def plain_body(slice_rows, row_owner, leaf_row, exponent, environment, ordering, sign_mask):
    tiles = lax.axis_size("tile")
    cut_count = lax.axis_size("cuts")
    width = slice_rows.shape[1]
    row_count = slice_rows.shape[0]
    capacity = max(2, (3 * row_count + 2 * tiles - 1) // (2 * tiles))
    factor = jnp.where(exponent == -1, 0.5, jnp.where(exponent == 1, 2.0, 1.0)).astype(jnp.float32)
    scaled = slice_rows * factor[:, None]
    owners = row_owner[:, 0]
    hits = (owners[:, None] == jnp.arange(tiles, dtype=jnp.int32)[None, :]).astype(jnp.int32)
    before = jnp.cumsum(hits, axis=0) - hits
    position = jnp.sum(before * hits, axis=1)
    placed = owners * capacity + position
    outgoing = jnp.zeros((tiles * capacity, width), jnp.float32).at[placed].set(scaled)
    outgoing_rows = jnp.zeros((tiles * capacity,), jnp.int32).at[placed].set(leaf_row)
    arrived, arrived_rows = (
        lax.all_to_all(outgoing, "tile", split_axis=0, concat_axis=0, tiled=True),
        lax.all_to_all(outgoing_rows, "tile", split_axis=0, concat_axis=0, tiled=True),
    )
    collected = jnp.zeros((width, width), jnp.float32).at[arrived_rows].add(arrived)
    contracted = multiply(collected, environment)
    columns = jnp.arange(width, dtype=jnp.int32)
    signs = 1.0 - 2.0 * sign_mask[0].astype(jnp.float32)
    signed = (ordering[0][:, None] == columns[None, :]).astype(jnp.float32) * signs[:, None]
    product = contracted + signed
    for level in range(tiles.bit_length() - 1):
        partner = from_partner(product, "tile", level)
        upper = lax.axis_index("tile") >> level & 1 == 1
        first_part = jnp.where(upper, partner, product)
        second_part = jnp.where(upper, product, partner)
        product = multiply(first_part, second_part)
    level = 0
    partner = from_partner(product, "cuts", level)
    upper = lax.axis_index("cuts") >> level & 1 == 1
    first_part = jnp.where(upper, partner, product)
    second_part = jnp.where(upper, product, partner)
    product = multiply(first_part, second_part)
    spread = jnp.sqrt(jnp.mean(product * product) + 1e-06)
    rows_each = width // tiles
    cols_each = width // cut_count
    row_start = lax.axis_index("tile") * rows_each
    col_start = lax.axis_index("cuts") * cols_each
    own_block = lax.dynamic_slice(product, (row_start, col_start), (rows_each, cols_each))
    return (own_block / spread, jnp.log(spread).reshape(1))


def solution(mesh):
    return jax.shard_map(
        body,
        mesh=mesh,
        in_specs=(
            P(("groups", "tile", "cuts"), None),
            P(("groups", "tile", "cuts"), None),
            P(("groups", "tile", "cuts")),
            P(("groups", "tile", "cuts")),
            P(("groups", "tile", "cuts"), None),
            P(("groups", "tile", "cuts"), None),
            P(("groups", "tile", "cuts"), None),
        ),
        out_specs=(P(("groups", "tile"), "cuts"), P("groups")),
        check_vma=False,
    )
```

```python
import functools

import jax
import jax.numpy as jnp
from jax import lax
from jax.experimental import pallas as pl
from jax.experimental.pallas import tpu as pltpu
from jax.sharding import PartitionSpec as P

MESH = pl.DeviceIdType.MESH
F32, BF16 = jnp.float32, jnp.bfloat16
NN = (((1,), (0,)), ((), ()))
NT = (((1,), (1,)), ((), ()))


def halves(x):
    high = x.astype(BF16)
    return high, (x - high.astype(F32)).astype(BF16)


def dot(a, b, dims=NN):
    return lax.dot_general(a, b, dims, preferred_element_type=F32)


def dot3(left, right, dims=NN):
    rows = left[0].shape[0]
    both = dot(jnp.concatenate(left, axis=0), right[0], dims)
    return (dot(left[0], right[1], dims) + both[rows:]) + both[:rows]


def kernel(tiles, cap, parts,
           rows_ref, owner_ref, leaf_row_ref, exponent_ref, env_ref, ordering_ref, sign_ref,
           block_ref, square_ref,
           rows_in, env_in, out_rows, out_ids, in_rows, in_ids, bond_out, bond_in, env_out, env_far,
           own, far, own_high, own_low, chain_high, chain_low,
           chain_in, chain_out, p_in, q_in, sums_out, sums_in,
           load, route_send, route_recv, far_send, far_recv, chain_send, chain_recv,
           p_send, p_recv, pass_send, pass_recv, q_send, q_recv, half_send, sum_send, sum_recv):
    group, me, cut = lax.axis_index("groups"), lax.axis_index("tile"), lax.axis_index("cuts")
    load_env = pltpu.make_async_copy(env_ref, env_in, load.at[0])
    load_rows = pltpu.make_async_copy(rows_ref, rows_in, load.at[1])
    load_env.start()
    load_rows.start()
    rows, width = rows_ref.shape
    step = width // tiles
    pairs = tiles // 2
    bits = pairs * parts
    bit_rows = step // parts
    slots = tiles * cap
    count = 2 * tiles
    ident = me * 2 + cut
    place = jnp.where(cut == 0, me, tiles - 1 - me)
    way = 1 - 2 * cut
    last = place == tiles - 1
    host = lax.rem(place, 2) == 1
    pair_me = me // 2

    def chunk(ref, k):
        return ref.at[pl.ds(pl.multiple_of(k * step, 8), step)]

    def part(ref, i):
        return ref.at[pl.ds(pl.multiple_of(i * bit_rows, 8), bit_rows)]

    def remote(src, dst, send, recv, tile, other):
        return pltpu.make_async_remote_copy(
            src_ref=src, dst_ref=dst, send_sem=send, recv_sem=recv,
            device_id=(group, tile, other), device_id_type=MESH)

    barrier = pltpu.get_barrier_semaphore()

    @pl.loop(1, count)
    def _(d):
        peer = lax.rem(ident + d, count)
        pl.semaphore_signal(barrier, inc=1, device_id=(group, peer // 2, lax.rem(peer, 2)), device_id_type=MESH)

    bond_out[0:1] = ordering_ref[...]
    bond_out[1:2] = sign_ref[...]
    load_env.wait()

    @pl.when(cut == 0)
    def _():
        env_out[...] = env_in[...]

    @pl.when(cut == 1)
    def _():
        env_out[...] = env_in[...].T

    def to_host():
        to = lax.rem(me + way + tiles, tiles)
        return (remote(bond_out, bond_in, far_send.at[0], far_recv.at[0], to, cut),
                remote(env_out, env_far, far_send.at[1], far_recv.at[1], to, cut))

    pl.semaphore_wait(barrier, count - 1)

    @pl.when(jnp.logical_not(host))
    def _():
        for copy in to_host():
            copy.start()

    load_rows.wait()
    level = exponent_ref[...]
    factor = jnp.where(level == -1, 0.5, jnp.where(level == 1, 2.0, 1.0)).astype(F32)
    factor = jnp.broadcast_to(factor, (128, rows)).T[:, 0:1]
    scaled = rows_in[...] * factor
    owner = owner_ref[...]
    hits = (owner == lax.broadcasted_iota(jnp.int32, (rows, 128), 1)).astype(F32)
    earlier = (lax.broadcasted_iota(jnp.int32, (rows, rows), 1)
               < lax.broadcasted_iota(jnp.int32, (rows, rows), 0)).astype(F32)
    before = dot(earlier.astype(BF16), hits.astype(BF16))
    position = jnp.sum(before * hits, axis=1, keepdims=True)
    position = jnp.broadcast_to(position, (rows, 128)).T[0:1, :].astype(jnp.int32)
    owner = jnp.broadcast_to(owner.astype(F32), (rows, 128)).T[0:1, :].astype(jnp.int32)
    slot = lax.broadcasted_iota(jnp.int32, (slots, rows), 0)
    pick = (slot == owner * cap + position).astype(F32).astype(BF16)
    high = scaled.astype(BF16)
    rest = scaled - high.astype(F32)
    middle = rest.astype(BF16)
    low = (rest - middle.astype(F32)).astype(BF16)
    out_rows[...] = ((dot(pick, low) + dot(pick, middle)) + dot(pick, high)).reshape(tiles, cap, width)
    seat = (slot == me * cap + position).astype(F32).astype(BF16)
    named = jnp.where(lax.broadcasted_iota(jnp.int32, (tiles, rows), 0) == owner,
                      leaf_row_ref[...] + 1, 0).astype(F32)
    named_high, named_low = halves(named)
    ids = dot(named_high, seat, NT) + dot(named_low, seat, NT)
    for t in range(tiles):
        out_ids[t] = ids[t:t + 1, :]

    def slots_of(source):
        return pl.ds(pl.multiple_of(source * cap, 8), cap)

    def route(pair, source):
        both = pl.ds(2 * pair, 2)
        to = 2 * pair + 1 - cut
        return (remote(out_rows.at[both], in_rows.at[:, slots_of(source)], route_send.at[0, pair],
                       route_recv.at[0, source], to, cut),
                remote(out_ids.at[both], in_ids.at[:, source], route_send.at[1, pair],
                       route_recv.at[1, source], to, cut))

    @pl.loop(1, pairs)
    def _(d):
        for copy in route(lax.rem(pair_me + d, pairs), me):
            copy.start()

    @pl.when(jnp.logical_not(host))
    def _():
        for copy in route(pair_me, me):
            copy.start()

    def bond_of(order, sign):
        return jnp.where(lax.broadcasted_iota(jnp.int32, (width, width), 0) == order,
                         (1 - 2 * sign).astype(F32), 0.0)

    @pl.when(host)
    def _():
        for c in range(2):
            in_rows[c, slots_of(me)] = out_rows[2 * pair_me + c]
            in_ids[c, me] = out_ids[2 * pair_me + c]
        to_host()[0].wait_recv()

        @pl.when(cut == 0)
        def _():
            own[...] = bond_of(bond_out[0:1], bond_out[1:2]).T
            far[...] = bond_of(bond_in[0:1], bond_in[1:2]).T

        @pl.when(cut == 1)
        def _():
            own[...] = bond_of(bond_out[0:1], bond_out[1:2])
            far[...] = bond_of(bond_in[0:1], bond_in[1:2])

        own_high[...], own_low[...] = halves(env_out[...])
        to_host()[1].wait_recv()
        chain_high[...], chain_low[...] = halves(env_far[...])

        @pl.loop(1, tiles)
        def _(d):
            source = lax.rem(me + d, tiles)
            for copy in route(pair_me, source):
                copy.wait_recv()

        def collected(c):
            wanted = jnp.sum(in_ids[c], axis=0).astype(jnp.int32) - 1
            spread_out = (lax.broadcasted_iota(jnp.int32, (width, slots), 0) == wanted).astype(F32).astype(BF16)
            in_high, in_low = halves(in_rows[c])
            return halves(dot(spread_out, in_low) + dot(spread_out, in_high))

        @pl.when(cut == 0)
        def _():
            own[...] += dot3(collected(1), (own_high[...], own_low[...]))
            far[...] += dot3(collected(0), (chain_high[...], chain_low[...]))

        @pl.when(cut == 1)
        def _():
            own[...] += dot3((own_high[...], own_low[...]), collected(0), NT)
            far[...] += dot3((chain_high[...], chain_low[...]), collected(1), NT)

        own_high[...], own_low[...] = halves(own[...])

    def link(k):
        return remote(chunk(chain_out, k), chunk(chain_in, k), chain_send.at[k], chain_recv.at[k],
                      lax.rem(me + 2 * way + tiles, tiles), cut)

    def p_copy(k):
        return remote(chunk(chain_out, k), p_in, p_send.at[k], p_recv.at[0], k, 0)

    def q_along(i):
        return remote(part(q_in, i), part(q_in, i), q_send.at[0, i], q_recv.at[i], lax.rem(me + 2, tiles), cut)

    def q_across(i):
        return remote(part(q_in, i), part(q_in, i), q_send.at[1, i], q_recv.at[i], lax.rem(me + 1, tiles), cut)

    def q_half(i):
        return remote(part(chain_out, i), part(q_in, i), half_send.at[i], q_recv.at[i], 0, 0)

    even_tile = lax.rem(me, 2) == 0
    p_root = jnp.logical_and(last, cut == 0)
    q_root = jnp.logical_and(last, cut == 1)

    def emit(k, value):
        at = pl.ds(pl.multiple_of(k * step, 8), step)

        @pl.when(jnp.logical_not(last))
        def _():
            chain_out[at] = value
            link(k).start()

        @pl.when(p_root)
        def _():
            @pl.when(k < tiles - 1)
            def _():
                chain_out[at] = value
                p_copy(k).start()

            @pl.when(k == tiles - 1)
            def _():
                p_in[...] = value

        @pl.when(q_root)
        def _():
            @pl.when(k < pairs)
            def _():
                chain_out[at] = value
                for i in range(parts):
                    q_half(k * parts + i).start()

            @pl.when(k >= pairs)
            def _():
                q_in[pl.ds(pl.multiple_of((k - pairs) * step, 8), step)] = value
                for i in range(parts):
                    q_along((k - pairs) * parts + i).start()
                    q_across((k - pairs) * parts + i).start()

    @pl.when(place == 1)
    def _():
        @pl.loop(0, tiles)
        def _(k):
            at = pl.ds(pl.multiple_of(k * step, 8), step)
            emit(k, dot3(halves(far[at]), (own_high[...], own_low[...])))

    @pl.when(jnp.logical_and(host, place > 1))
    def _():
        chain_high[...], chain_low[...] = halves(dot3(halves(far[...]), (own_high[...], own_low[...])))

        @pl.loop(0, tiles)
        def _(k):
            at = pl.ds(pl.multiple_of(k * step, 8), step)
            link(k).wait_recv()
            emit(k, dot3(halves(chain_in[at]), (chain_high[...], chain_low[...])))

    @pl.when(jnp.logical_not(q_root))
    def _():
        @pl.loop(0, bits)
        def _(k):
            q_half(k).wait_recv()

            @pl.when(even_tile)
            def _():
                @pl.when(me < tiles - 2)
                def _():
                    q_along(k).start()

                q_across(k).start()

    def p_pass():
        return remote(p_in, p_in, pass_send.at[0], pass_recv.at[0], me, 1)

    @pl.when(cut == 0)
    def _():
        @pl.when(jnp.logical_not(p_root))
        def _():
            p_copy(0).wait_recv()

        p_pass().start()

    @pl.when(cut == 1)
    def _():
        p_pass().wait_recv()

    result = dot3(halves(p_in[...]), halves(q_in[...]), NT)
    block_ref[...] = result
    total = jnp.sum(jnp.sum(result * result, axis=0, keepdims=True), axis=1, keepdims=True)
    total = jnp.broadcast_to(total, (8, 128))
    sums_out[...] = total

    def share(peer, slot):
        return remote(sums_out, sums_in.at[slot], sum_send.at[peer], sum_recv.at[slot],
                      peer // 2, lax.rem(peer, 2))

    @pl.loop(1, count)
    def _(d):
        share(lax.rem(ident + d, count), ident).start()

    sums_in[ident] = total

    @pl.loop(1, pairs)
    def _(d):
        for copy in route(lax.rem(pair_me + d, pairs), me):
            copy.wait_send()

    @pl.when(jnp.logical_not(host))
    def _():
        for copy in route(pair_me, me) + to_host():
            copy.wait_send()

    @pl.when(jnp.logical_and(host, jnp.logical_not(last)))
    def _():
        @pl.loop(0, tiles)
        def _(k):
            link(k).wait_send()

    @pl.when(p_root)
    def _():
        @pl.loop(0, tiles - 1)
        def _(k):
            p_copy(k).wait_send()

    @pl.when(q_root)
    def _():
        @pl.loop(0, bits)
        def _(k):
            q_half(k).wait_send()

    @pl.when(even_tile)
    def _():
        @pl.loop(0, bits)
        def _(k):
            @pl.when(me < tiles - 2)
            def _():
                q_along(k).wait_send()

            q_across(k).wait_send()

    @pl.when(cut == 0)
    def _():
        p_pass().wait_send()

    @pl.loop(1, count)
    def _(d):
        peer = lax.rem(ident + d, count)
        share(peer, peer).wait_recv()
        share(peer, peer).wait_send()

    square_ref[...] = jnp.sum(sums_in[...], axis=0)


def body(slice_rows, row_owner, leaf_row, exponent, environment, ordering, sign_mask):
    tiles = lax.axis_size("tile")
    rows, width = slice_rows.shape
    step = width // tiles
    half = width // 2
    cap = max(2, (3 * rows + 2 * tiles - 1) // (2 * tiles))
    cap = (cap + 15) // 16 * 16
    slots = tiles * cap
    count = 2 * tiles
    parts = 2 if step % 32 == 0 else 1
    bits = tiles // 2 * parts
    vmem, dma = pltpu.VMEM, pltpu.SemaphoreType.DMA
    block, square = pl.pallas_call(
        functools.partial(kernel, tiles, cap, parts),
        out_shape=(jax.ShapeDtypeStruct((step, half), F32), jax.ShapeDtypeStruct((8, 128), F32)),
        in_specs=[pl.BlockSpec(memory_space=pl.ANY if i in (0, 4) else vmem) for i in range(7)],
        out_specs=(pl.BlockSpec(memory_space=vmem), pl.BlockSpec(memory_space=vmem)),
        scratch_shapes=[
            vmem((rows, width), F32), vmem((width, width), F32),
            vmem((tiles, cap, width), F32), vmem((tiles, 1, slots), F32),
            vmem((2, slots, width), F32), vmem((2, tiles, 1, slots), F32),
            vmem((2, width), jnp.int32), vmem((2, width), jnp.int32),
            vmem((width, width), F32), vmem((width, width), F32),
            vmem((width, width), F32), vmem((width, width), F32),
            vmem((width, width), BF16), vmem((width, width), BF16),
            vmem((width, width), BF16), vmem((width, width), BF16),
            vmem((width, width), F32), vmem((width, width), F32),
            vmem((step, width), F32), vmem((half, width), F32),
            vmem((8, 128), F32), vmem((count, 8, 128), F32),
            dma((2,)), dma((2, tiles // 2)), dma((2, tiles)), dma((2,)), dma((2,)), dma((tiles,)), dma((tiles,)),
            dma((tiles,)), dma((1,)), dma((1,)), dma((1,)),
            dma((2, bits)), dma((bits,)), dma((bits,)), dma((count,)), dma((count,)),
        ],
        compiler_params=pltpu.CompilerParams(
            collective_id=0, has_side_effects=True, vmem_limit_bytes=60 * 1024 * 1024),
    )(slice_rows, row_owner, leaf_row.reshape(1, rows), exponent.reshape(1, rows),
      environment, ordering, sign_mask)
    spread = jnp.sqrt(square[0, 0] / (width * width) + 1e-06)
    return block / spread, jnp.log(spread).reshape(1)


def from_partner(x, axis, bit):
    return lax.ppermute(x, axis, [(i, i ^ 1 << bit) for i in range(lax.axis_size(axis))])


def multiply(left_factor, right_factor):
    return jnp.dot(
        left_factor,
        right_factor,
        precision=lax.Precision.HIGHEST,
        preferred_element_type=jnp.float32,
    )


def plain_body(slice_rows, row_owner, leaf_row, exponent, environment, ordering, sign_mask):
    tiles = lax.axis_size("tile")
    cut_count = lax.axis_size("cuts")
    width = slice_rows.shape[1]
    row_count = slice_rows.shape[0]
    capacity = max(2, (3 * row_count + 2 * tiles - 1) // (2 * tiles))
    factor = jnp.where(exponent == -1, 0.5, jnp.where(exponent == 1, 2.0, 1.0)).astype(jnp.float32)
    scaled = slice_rows * factor[:, None]
    owners = row_owner[:, 0]
    hits = (owners[:, None] == jnp.arange(tiles, dtype=jnp.int32)[None, :]).astype(jnp.int32)
    before = jnp.cumsum(hits, axis=0) - hits
    position = jnp.sum(before * hits, axis=1)
    placed = owners * capacity + position
    outgoing = jnp.zeros((tiles * capacity, width), jnp.float32).at[placed].set(scaled)
    outgoing_rows = jnp.zeros((tiles * capacity,), jnp.int32).at[placed].set(leaf_row)
    arrived, arrived_rows = (
        lax.all_to_all(outgoing, "tile", split_axis=0, concat_axis=0, tiled=True),
        lax.all_to_all(outgoing_rows, "tile", split_axis=0, concat_axis=0, tiled=True),
    )
    collected = jnp.zeros((width, width), jnp.float32).at[arrived_rows].add(arrived)
    contracted = multiply(collected, environment)
    columns = jnp.arange(width, dtype=jnp.int32)
    signs = 1.0 - 2.0 * sign_mask[0].astype(jnp.float32)
    signed = (ordering[0][:, None] == columns[None, :]).astype(jnp.float32) * signs[:, None]
    product = contracted + signed
    for level in range(tiles.bit_length() - 1):
        partner = from_partner(product, "tile", level)
        upper = lax.axis_index("tile") >> level & 1 == 1
        first_part = jnp.where(upper, partner, product)
        second_part = jnp.where(upper, product, partner)
        product = multiply(first_part, second_part)
    level = 0
    partner = from_partner(product, "cuts", level)
    upper = lax.axis_index("cuts") >> level & 1 == 1
    first_part = jnp.where(upper, partner, product)
    second_part = jnp.where(upper, product, partner)
    product = multiply(first_part, second_part)
    spread = jnp.sqrt(jnp.mean(product * product) + 1e-06)
    rows_each = width // tiles
    cols_each = width // cut_count
    row_start = lax.axis_index("tile") * rows_each
    col_start = lax.axis_index("cuts") * cols_each
    own_block = lax.dynamic_slice(product, (row_start, col_start), (rows_each, cols_each))
    return (own_block / spread, jnp.log(spread).reshape(1))


def solution(mesh):
    tiles, cuts = mesh.shape["tile"], mesh.shape["cuts"]
    fits = cuts == 2 and 4 <= tiles <= 16
    return jax.shard_map(
        body if fits else plain_body,
        mesh=mesh,
        in_specs=(
            P(("groups", "tile", "cuts"), None),
            P(("groups", "tile", "cuts"), None),
            P(("groups", "tile", "cuts")),
            P(("groups", "tile", "cuts")),
            P(("groups", "tile", "cuts"), None),
            P(("groups", "tile", "cuts"), None),
            P(("groups", "tile", "cuts"), None),
        ),
        out_specs=(P(("groups", "tile"), "cuts"), P("groups")),
        check_vma=False,
    )
```

```python
import functools

import jax
import jax.numpy as jnp
from jax import lax
from jax.experimental import pallas as pl
from jax.experimental.pallas import tpu as pltpu
from jax.sharding import PartitionSpec as P

MESH = pl.DeviceIdType.MESH
F32, BF16 = jnp.float32, jnp.bfloat16
NN = (((1,), (0,)), ((), ()))
NT = (((1,), (1,)), ((), ()))


def halves(x):
    high = x.astype(BF16)
    return high, (x - high.astype(F32)).astype(BF16)


def dot(a, b, dims=NN):
    return lax.dot_general(a, b, dims, preferred_element_type=F32)


def dot3(left, right, dims=NN):
    return (dot(left[0], right[1], dims) + dot(left[1], right[0], dims)) + dot(left[0], right[0], dims)


def kernel(tiles, cap, parts,
           rows_ref, owner_ref, leaf_row_ref, exponent_ref, env_ref, ordering_ref, sign_ref,
           block_ref, square_ref,
           rows_in, env_in, out_rows, out_ids, in_rows, in_ids, bond_out, bond_in, env_out, env_far,
           own, far, own_high, own_low, chain_high, chain_low,
           chain_in, chain_out, p_in, q_in, sums_out, sums_in,
           load, route_send, route_recv, far_send, far_recv, chain_send, chain_recv,
           p_send, p_recv, pass_send, pass_recv, q_send, q_recv, half_send, sum_send, sum_recv):
    group, me, cut = lax.axis_index("groups"), lax.axis_index("tile"), lax.axis_index("cuts")
    load_env = pltpu.make_async_copy(env_ref, env_in, load.at[0])
    load_rows = pltpu.make_async_copy(rows_ref, rows_in, load.at[1])
    load_env.start()
    load_rows.start()
    rows, width = rows_ref.shape
    step = width // tiles
    pairs = tiles // 2
    bits = pairs * parts
    bit_rows = step // parts
    slots = tiles * cap
    count = 2 * tiles
    ident = me * 2 + cut
    place = jnp.where(cut == 0, me, tiles - 1 - me)
    way = 1 - 2 * cut
    last = place == tiles - 1
    host = lax.rem(place, 2) == 1
    pair_me = me // 2

    def chunk(ref, k):
        return ref.at[pl.ds(pl.multiple_of(k * step, 8), step)]

    def part(ref, i):
        return ref.at[pl.ds(pl.multiple_of(i * bit_rows, 8), bit_rows)]

    def remote(src, dst, send, recv, tile, other):
        return pltpu.make_async_remote_copy(
            src_ref=src, dst_ref=dst, send_sem=send, recv_sem=recv,
            device_id=(group, tile, other), device_id_type=MESH)

    barrier = pltpu.get_barrier_semaphore()

    @pl.loop(1, count)
    def _(d):
        peer = lax.rem(ident + d, count)
        pl.semaphore_signal(barrier, inc=1, device_id=(group, peer // 2, lax.rem(peer, 2)), device_id_type=MESH)

    bond_out[0:1] = ordering_ref[...]
    bond_out[1:2] = sign_ref[...]
    load_env.wait()

    @pl.when(cut == 0)
    def _():
        env_out[...] = env_in[...]

    @pl.when(cut == 1)
    def _():
        env_out[...] = env_in[...].T

    def to_host():
        to = lax.rem(me + way + tiles, tiles)
        return (remote(bond_out, bond_in, far_send.at[0], far_recv.at[0], to, cut),
                remote(env_out.at[:width // 2], env_far.at[:width // 2], far_send.at[1], far_recv.at[1], to, cut),
                remote(env_out.at[width // 2:], env_far.at[width // 2:], far_send.at[2], far_recv.at[2], to, cut))

    pl.semaphore_wait(barrier, count - 1)

    @pl.when(jnp.logical_not(host))
    def _():
        for copy in to_host()[:2]:
            copy.start()

    load_rows.wait()
    level = exponent_ref[...]
    factor = jnp.where(level == -1, 0.5, jnp.where(level == 1, 2.0, 1.0)).astype(F32)
    factor = jnp.broadcast_to(factor, (128, rows)).T[:, 0:1]
    scaled = rows_in[...] * factor
    owner = owner_ref[...]
    hits = (owner == lax.broadcasted_iota(jnp.int32, (rows, 128), 1)).astype(F32)
    earlier = (lax.broadcasted_iota(jnp.int32, (rows, rows), 1)
               < lax.broadcasted_iota(jnp.int32, (rows, rows), 0)).astype(F32)
    before = dot(earlier.astype(BF16), hits.astype(BF16))
    position = jnp.sum(before * hits, axis=1, keepdims=True)
    position = jnp.broadcast_to(position, (rows, 128)).T[0:1, :].astype(jnp.int32)
    owner = jnp.broadcast_to(owner.astype(F32), (rows, 128)).T[0:1, :].astype(jnp.int32)
    slot = lax.broadcasted_iota(jnp.int32, (slots, rows), 0)
    pick = (slot == owner * cap + position).astype(F32).astype(BF16)
    high = scaled.astype(BF16)
    rest = scaled - high.astype(F32)
    middle = rest.astype(BF16)
    low = (rest - middle.astype(F32)).astype(BF16)
    out_rows[...] = ((dot(pick, low) + dot(pick, middle)) + dot(pick, high)).reshape(tiles, cap, width)
    seat = (slot == me * cap + position).astype(F32).astype(BF16)
    named = jnp.where(lax.broadcasted_iota(jnp.int32, (tiles, rows), 0) == owner,
                      leaf_row_ref[...] + 1, 0).astype(F32)
    named_high, named_low = halves(named)
    ids = dot(named_high, seat, NT) + dot(named_low, seat, NT)
    for t in range(tiles):
        out_ids[t] = ids[t:t + 1, :]

    def slots_of(source):
        return pl.ds(pl.multiple_of(source * cap, 8), cap)

    def route(pair, source):
        both = pl.ds(2 * pair, 2)
        to = 2 * pair + 1 - cut
        return (remote(out_rows.at[both], in_rows.at[:, slots_of(source)], route_send.at[0, pair],
                       route_recv.at[0, source], to, cut),
                remote(out_ids.at[both], in_ids.at[:, source], route_send.at[1, pair],
                       route_recv.at[1, source], to, cut))

    @pl.loop(1, pairs)
    def _(d):
        for copy in route(lax.rem(pair_me + d, pairs), me):
            copy.start()

    @pl.when(jnp.logical_not(host))
    def _():
        for copy in route(pair_me, me) + to_host()[2:]:
            copy.start()

    def bond_of(order, sign):
        return jnp.where(lax.broadcasted_iota(jnp.int32, (width, width), 0) == order,
                         (1 - 2 * sign).astype(F32), 0.0)

    @pl.when(host)
    def _():
        for c in range(2):
            in_rows[c, slots_of(me)] = out_rows[2 * pair_me + c]
            in_ids[c, me] = out_ids[2 * pair_me + c]
        to_host()[0].wait_recv()

        @pl.when(cut == 0)
        def _():
            own[...] = bond_of(bond_out[0:1], bond_out[1:2]).T
            far[...] = bond_of(bond_in[0:1], bond_in[1:2]).T

        @pl.when(cut == 1)
        def _():
            own[...] = bond_of(bond_out[0:1], bond_out[1:2])
            far[...] = bond_of(bond_in[0:1], bond_in[1:2])

        own_high[...], own_low[...] = halves(env_out[...])
        @pl.loop(1, tiles)
        def _(d):
            source = lax.rem(me + d, tiles)
            for copy in route(pair_me, source):
                copy.wait_recv()

        def collected(c):
            wanted = jnp.sum(in_ids[c], axis=0).astype(jnp.int32) - 1
            spread_out = (lax.broadcasted_iota(jnp.int32, (width, slots), 0) == wanted).astype(F32).astype(BF16)
            in_high, in_low = halves(in_rows[c])
            return halves(dot(spread_out, in_low) + dot(spread_out, in_high))

        @pl.when(cut == 0)
        def _():
            own[...] += dot3(collected(1), (own_high[...], own_low[...]))

        @pl.when(cut == 1)
        def _():
            own[...] += dot3((own_high[...], own_low[...]), collected(0), NT)

        own_high[...], own_low[...] = halves(own[...])
        for copy in to_host()[1:]:
            copy.wait_recv()
        chain_high[...], chain_low[...] = halves(env_far[...])

        @pl.when(cut == 0)
        def _():
            far[...] += dot3(collected(0), (chain_high[...], chain_low[...]))

        @pl.when(cut == 1)
        def _():
            far[...] += dot3((chain_high[...], chain_low[...]), collected(1), NT)


    def link(k):
        return remote(chunk(chain_out, k), chunk(chain_in, k), chain_send.at[k], chain_recv.at[k],
                      lax.rem(me + 2 * way + tiles, tiles), cut)

    def p_copy(k):
        return remote(chunk(chain_out, k), p_in, p_send.at[k], p_recv.at[0], k, 0)

    def q_along(i):
        return remote(part(q_in, i), part(q_in, i), q_send.at[0, i], q_recv.at[i], lax.rem(me + 2, tiles), cut)

    def q_across(i):
        return remote(part(q_in, i), part(q_in, i), q_send.at[1, i], q_recv.at[i], lax.rem(me + 1, tiles), cut)

    def q_half(i):
        return remote(part(chain_out, i), part(q_in, i), half_send.at[i], q_recv.at[i], 0, 0)

    even_tile = lax.rem(me, 2) == 0
    p_root = jnp.logical_and(last, cut == 0)
    q_root = jnp.logical_and(last, cut == 1)

    def emit(k, value):
        at = pl.ds(pl.multiple_of(k * step, 8), step)

        @pl.when(jnp.logical_not(last))
        def _():
            chain_out[at] = value
            link(k).start()

        @pl.when(p_root)
        def _():
            @pl.when(k < tiles - 1)
            def _():
                chain_out[at] = value
                p_copy(k).start()

            @pl.when(k == tiles - 1)
            def _():
                p_in[...] = value

        @pl.when(q_root)
        def _():
            @pl.when(k < pairs)
            def _():
                chain_out[at] = value
                for i in range(parts):
                    q_half(k * parts + i).start()

            @pl.when(k >= pairs)
            def _():
                q_in[pl.ds(pl.multiple_of((k - pairs) * step, 8), step)] = value
                for i in range(parts):
                    q_along((k - pairs) * parts + i).start()
                    q_across((k - pairs) * parts + i).start()

    @pl.when(place == 1)
    def _():
        @pl.loop(0, tiles)
        def _(k):
            at = pl.ds(pl.multiple_of(k * step, 8), step)
            emit(k, dot3(halves(far[at]), (own_high[...], own_low[...])))

    @pl.when(jnp.logical_and(host, place > 1))
    def _():
        chain_high[...], chain_low[...] = halves(dot3(halves(far[...]), (own_high[...], own_low[...])))

        @pl.loop(0, tiles)
        def _(k):
            at = pl.ds(pl.multiple_of(k * step, 8), step)
            link(k).wait_recv()
            emit(k, dot3(halves(chain_in[at]), (chain_high[...], chain_low[...])))

    @pl.when(jnp.logical_not(q_root))
    def _():
        @pl.loop(0, bits)
        def _(k):
            q_half(k).wait_recv()

            @pl.when(even_tile)
            def _():
                @pl.when(me < tiles - 2)
                def _():
                    q_along(k).start()

                q_across(k).start()

    def p_pass():
        return remote(p_in, p_in, pass_send.at[0], pass_recv.at[0], me, 1)

    @pl.when(cut == 0)
    def _():
        @pl.when(jnp.logical_not(p_root))
        def _():
            p_copy(0).wait_recv()

        p_pass().start()

    @pl.when(cut == 1)
    def _():
        p_pass().wait_recv()

    result = dot3(halves(p_in[...]), halves(q_in[...]), NT)
    block_ref[...] = result
    total = jnp.sum(jnp.sum(result * result, axis=0, keepdims=True), axis=1, keepdims=True)
    total = jnp.broadcast_to(total, (8, 128))
    sums_out[...] = total

    def share(peer, slot):
        return remote(sums_out, sums_in.at[slot], sum_send.at[peer], sum_recv.at[slot],
                      peer // 2, lax.rem(peer, 2))

    @pl.loop(1, count)
    def _(d):
        share(lax.rem(ident + d, count), ident).start()

    sums_in[ident] = total

    @pl.loop(1, pairs)
    def _(d):
        for copy in route(lax.rem(pair_me + d, pairs), me):
            copy.wait_send()

    @pl.when(jnp.logical_not(host))
    def _():
        for copy in route(pair_me, me) + to_host():
            copy.wait_send()

    @pl.when(jnp.logical_and(host, jnp.logical_not(last)))
    def _():
        @pl.loop(0, tiles)
        def _(k):
            link(k).wait_send()

    @pl.when(p_root)
    def _():
        @pl.loop(0, tiles - 1)
        def _(k):
            p_copy(k).wait_send()

    @pl.when(q_root)
    def _():
        @pl.loop(0, bits)
        def _(k):
            q_half(k).wait_send()

    @pl.when(even_tile)
    def _():
        @pl.loop(0, bits)
        def _(k):
            @pl.when(me < tiles - 2)
            def _():
                q_along(k).wait_send()

            q_across(k).wait_send()

    @pl.when(cut == 0)
    def _():
        p_pass().wait_send()

    @pl.loop(1, count)
    def _(d):
        peer = lax.rem(ident + d, count)
        share(peer, peer).wait_recv()
        share(peer, peer).wait_send()

    square_ref[...] = jnp.sum(sums_in[...], axis=0)


def body(slice_rows, row_owner, leaf_row, exponent, environment, ordering, sign_mask):
    tiles = lax.axis_size("tile")
    rows, width = slice_rows.shape
    step = width // tiles
    half = width // 2
    cap = max(2, (3 * rows + 2 * tiles - 1) // (2 * tiles))
    cap = (cap + 15) // 16 * 16
    slots = tiles * cap
    count = 2 * tiles
    parts = 2 if step % 32 == 0 else 1
    bits = tiles // 2 * parts
    vmem, dma = pltpu.VMEM, pltpu.SemaphoreType.DMA
    block, square = pl.pallas_call(
        functools.partial(kernel, tiles, cap, parts),
        out_shape=(jax.ShapeDtypeStruct((step, half), F32), jax.ShapeDtypeStruct((8, 128), F32)),
        in_specs=[pl.BlockSpec(memory_space=pl.ANY if i in (0, 4) else vmem) for i in range(7)],
        out_specs=(pl.BlockSpec(memory_space=vmem), pl.BlockSpec(memory_space=vmem)),
        scratch_shapes=[
            vmem((rows, width), F32), vmem((width, width), F32),
            vmem((tiles, cap, width), F32), vmem((tiles, 1, slots), F32),
            vmem((2, slots, width), F32), vmem((2, tiles, 1, slots), F32),
            vmem((2, width), jnp.int32), vmem((2, width), jnp.int32),
            vmem((width, width), F32), vmem((width, width), F32),
            vmem((width, width), F32), vmem((width, width), F32),
            vmem((width, width), BF16), vmem((width, width), BF16),
            vmem((width, width), BF16), vmem((width, width), BF16),
            vmem((width, width), F32), vmem((width, width), F32),
            vmem((step, width), F32), vmem((half, width), F32),
            vmem((8, 128), F32), vmem((count, 8, 128), F32),
            dma((2,)), dma((2, tiles // 2)), dma((2, tiles)), dma((3,)), dma((3,)), dma((tiles,)), dma((tiles,)),
            dma((tiles,)), dma((1,)), dma((1,)), dma((1,)),
            dma((2, bits)), dma((bits,)), dma((bits,)), dma((count,)), dma((count,)),
        ],
        compiler_params=pltpu.CompilerParams(
            collective_id=0, has_side_effects=True, vmem_limit_bytes=40 * 1024 * 1024),
    )(slice_rows, row_owner, leaf_row.reshape(1, rows), exponent.reshape(1, rows),
      environment, ordering, sign_mask)
    spread = jnp.sqrt(square[0, 0] / (width * width) + 1e-06)
    return block / spread, jnp.log(spread).reshape(1)


def from_partner(x, axis, bit):
    return lax.ppermute(x, axis, [(i, i ^ 1 << bit) for i in range(lax.axis_size(axis))])


def multiply(left_factor, right_factor):
    return jnp.dot(
        left_factor,
        right_factor,
        precision=lax.Precision.HIGHEST,
        preferred_element_type=jnp.float32,
    )


def plain_body(slice_rows, row_owner, leaf_row, exponent, environment, ordering, sign_mask):
    tiles = lax.axis_size("tile")
    cut_count = lax.axis_size("cuts")
    width = slice_rows.shape[1]
    row_count = slice_rows.shape[0]
    capacity = max(2, (3 * row_count + 2 * tiles - 1) // (2 * tiles))
    factor = jnp.where(exponent == -1, 0.5, jnp.where(exponent == 1, 2.0, 1.0)).astype(jnp.float32)
    scaled = slice_rows * factor[:, None]
    owners = row_owner[:, 0]
    hits = (owners[:, None] == jnp.arange(tiles, dtype=jnp.int32)[None, :]).astype(jnp.int32)
    before = jnp.cumsum(hits, axis=0) - hits
    position = jnp.sum(before * hits, axis=1)
    placed = owners * capacity + position
    outgoing = jnp.zeros((tiles * capacity, width), jnp.float32).at[placed].set(scaled)
    outgoing_rows = jnp.zeros((tiles * capacity,), jnp.int32).at[placed].set(leaf_row)
    arrived, arrived_rows = (
        lax.all_to_all(outgoing, "tile", split_axis=0, concat_axis=0, tiled=True),
        lax.all_to_all(outgoing_rows, "tile", split_axis=0, concat_axis=0, tiled=True),
    )
    collected = jnp.zeros((width, width), jnp.float32).at[arrived_rows].add(arrived)
    contracted = multiply(collected, environment)
    columns = jnp.arange(width, dtype=jnp.int32)
    signs = 1.0 - 2.0 * sign_mask[0].astype(jnp.float32)
    signed = (ordering[0][:, None] == columns[None, :]).astype(jnp.float32) * signs[:, None]
    product = contracted + signed
    for level in range(tiles.bit_length() - 1):
        partner = from_partner(product, "tile", level)
        upper = lax.axis_index("tile") >> level & 1 == 1
        first_part = jnp.where(upper, partner, product)
        second_part = jnp.where(upper, product, partner)
        product = multiply(first_part, second_part)
    level = 0
    partner = from_partner(product, "cuts", level)
    upper = lax.axis_index("cuts") >> level & 1 == 1
    first_part = jnp.where(upper, partner, product)
    second_part = jnp.where(upper, product, partner)
    product = multiply(first_part, second_part)
    spread = jnp.sqrt(jnp.mean(product * product) + 1e-06)
    rows_each = width // tiles
    cols_each = width // cut_count
    row_start = lax.axis_index("tile") * rows_each
    col_start = lax.axis_index("cuts") * cols_each
    own_block = lax.dynamic_slice(product, (row_start, col_start), (rows_each, cols_each))
    return (own_block / spread, jnp.log(spread).reshape(1))


def solution(mesh):
    tiles, cuts = mesh.shape["tile"], mesh.shape["cuts"]
    fits = cuts == 2 and 4 <= tiles <= 16
    return jax.shard_map(
        body if fits else plain_body,
        mesh=mesh,
        in_specs=(
            P(("groups", "tile", "cuts"), None),
            P(("groups", "tile", "cuts"), None),
            P(("groups", "tile", "cuts")),
            P(("groups", "tile", "cuts")),
            P(("groups", "tile", "cuts"), None),
            P(("groups", "tile", "cuts"), None),
            P(("groups", "tile", "cuts"), None),
        ),
        out_specs=(P(("groups", "tile"), "cuts"), P("groups")),
        check_vma=False,
    )
```

```python
import functools

import jax
import jax.numpy as jnp
from jax import lax
from jax.experimental import pallas as pl
from jax.experimental.pallas import tpu as pltpu
from jax.sharding import PartitionSpec as P

MESH = pl.DeviceIdType.MESH
F32, BF16 = jnp.float32, jnp.bfloat16
NN = (((1,), (0,)), ((), ()))
NT = (((1,), (1,)), ((), ()))


def halves(x):
    high = x.astype(BF16)
    return high, (x - high.astype(F32)).astype(BF16)


def dot(a, b, dims=NN):
    return lax.dot_general(a, b, dims, preferred_element_type=F32)


def dot3(left, right, dims=NN):
    return (dot(left[0], right[1], dims) + dot(left[1], right[0], dims)) + dot(left[0], right[0], dims)


def kernel(tiles, cap, parts,
           rows_ref, owner_ref, leaf_row_ref, exponent_ref, env_ref, ordering_ref, sign_ref,
           block_ref, square_ref,
           rows_in, env_in, out_rows, out_ids, in_rows, in_ids, bond_out, bond_in, env_out, env_far,
           own, far, own_high, own_low, chain_high, chain_low,
           chain_in, chain_out, p_in, q_in, sums_out, sums_in,
           load, route_send, route_recv, far_send, far_recv, chain_send, chain_recv,
           p_send, p_recv, pass_send, pass_recv, q_send, q_recv, half_send, sum_send, sum_recv):
    group, me, cut = lax.axis_index("groups"), lax.axis_index("tile"), lax.axis_index("cuts")
    load_env = pltpu.make_async_copy(env_ref, env_in, load.at[0])
    load_rows = pltpu.make_async_copy(rows_ref, rows_in, load.at[1])
    load_env.start()
    load_rows.start()
    rows, width = rows_ref.shape
    step = width // tiles
    pairs = tiles // 2
    bits = pairs * parts
    bit_rows = step // parts
    slots = tiles * cap
    count = 2 * tiles
    ident = me * 2 + cut
    place = jnp.where(cut == 0, me, tiles - 1 - me)
    way = 1 - 2 * cut
    last = place == tiles - 1
    host = lax.rem(place, 2) == 1
    pair_me = me // 2

    def chunk(ref, k):
        return ref.at[pl.ds(pl.multiple_of(k * step, 8), step)]

    def part(ref, i):
        return ref.at[pl.ds(pl.multiple_of(i * bit_rows, 8), bit_rows)]

    def remote(src, dst, send, recv, tile, other):
        return pltpu.make_async_remote_copy(
            src_ref=src, dst_ref=dst, send_sem=send, recv_sem=recv,
            device_id=(group, tile, other), device_id_type=MESH)

    barrier = pltpu.get_barrier_semaphore()

    @pl.loop(1, count)
    def _(d):
        peer = lax.rem(ident + d, count)
        pl.semaphore_signal(barrier, inc=1, device_id=(group, peer // 2, lax.rem(peer, 2)), device_id_type=MESH)

    bond_out[0:1] = ordering_ref[...]
    bond_out[1:2] = sign_ref[...]
    load_env.wait()

    @pl.when(cut == 0)
    def _():
        env_out[...] = env_in[...]

    @pl.when(cut == 1)
    def _():
        env_out[...] = env_in[...].T

    def to_host():
        to = lax.rem(me + way + tiles, tiles)
        return (remote(bond_out, bond_in, far_send.at[0], far_recv.at[0], to, cut),
                remote(env_out.at[:width // 2], env_far.at[:width // 2], far_send.at[1], far_recv.at[1], to, cut),
                remote(env_out.at[width // 2:], env_far.at[width // 2:], far_send.at[2], far_recv.at[2], to, cut))

    pl.semaphore_wait(barrier, count - 1)

    @pl.when(jnp.logical_not(host))
    def _():
        for copy in to_host()[:2]:
            copy.start()

    load_rows.wait()
    level = exponent_ref[...]
    factor = jnp.where(level == -1, 0.5, jnp.where(level == 1, 2.0, 1.0)).astype(F32)
    factor = jnp.broadcast_to(factor, (128, rows)).T[:, 0:1]
    scaled = rows_in[...] * factor
    owner = owner_ref[...]
    hits = (owner == lax.broadcasted_iota(jnp.int32, (rows, 128), 1)).astype(F32)
    earlier = (lax.broadcasted_iota(jnp.int32, (rows, rows), 1)
               < lax.broadcasted_iota(jnp.int32, (rows, rows), 0)).astype(F32)
    before = dot(earlier.astype(BF16), hits.astype(BF16))
    position = jnp.sum(before * hits, axis=1, keepdims=True)
    position = jnp.broadcast_to(position, (rows, 128)).T[0:1, :].astype(jnp.int32)
    owner = jnp.broadcast_to(owner.astype(F32), (rows, 128)).T[0:1, :].astype(jnp.int32)
    slot = lax.broadcasted_iota(jnp.int32, (slots, rows), 0)
    pick = (slot == owner * cap + position).astype(F32).astype(BF16)
    high = scaled.astype(BF16)
    rest = scaled - high.astype(F32)
    middle = rest.astype(BF16)
    low = (rest - middle.astype(F32)).astype(BF16)
    out_rows[...] = ((dot(pick, low) + dot(pick, middle)) + dot(pick, high)).reshape(tiles, cap, width)
    seat = (slot == me * cap + position).astype(F32).astype(BF16)
    named = jnp.where(lax.broadcasted_iota(jnp.int32, (tiles, rows), 0) == owner,
                      leaf_row_ref[...] + 1, 0).astype(F32)
    named_high, named_low = halves(named)
    ids = dot(named_high, seat, NT) + dot(named_low, seat, NT)
    for t in range(tiles):
        out_ids[t] = ids[t:t + 1, :]

    def slots_of(source):
        return pl.ds(pl.multiple_of(source * cap, 8), cap)

    def route(pair, source):
        both = pl.ds(2 * pair, 2)
        to = 2 * pair + 1 - cut
        return (remote(out_rows.at[both], in_rows.at[:, slots_of(source)], route_send.at[0, pair],
                       route_recv.at[0, source], to, cut),
                remote(out_ids.at[both], in_ids.at[:, source], route_send.at[1, pair],
                       route_recv.at[1, source], to, cut))

    @pl.loop(1, pairs)
    def _(d):
        for copy in route(lax.rem(pair_me + d, pairs), me):
            copy.start()

    @pl.when(jnp.logical_not(host))
    def _():
        for copy in route(pair_me, me) + to_host()[2:]:
            copy.start()

    def bond_of(order, sign):
        return jnp.where(lax.broadcasted_iota(jnp.int32, (width, width), 0) == order,
                         (1 - 2 * sign).astype(F32), 0.0)

    @pl.when(host)
    def _():
        for c in range(2):
            in_rows[c, slots_of(me)] = out_rows[2 * pair_me + c]
            in_ids[c, me] = out_ids[2 * pair_me + c]
        to_host()[0].wait_recv()

        @pl.when(cut == 0)
        def _():
            own[...] = bond_of(bond_out[0:1], bond_out[1:2]).T
            far[...] = bond_of(bond_in[0:1], bond_in[1:2]).T

        @pl.when(cut == 1)
        def _():
            own[...] = bond_of(bond_out[0:1], bond_out[1:2])
            far[...] = bond_of(bond_in[0:1], bond_in[1:2])

        own_high[...], own_low[...] = halves(env_out[...])
        @pl.loop(1, tiles)
        def _(d):
            source = lax.rem(me + d, tiles)
            for copy in route(pair_me, source):
                copy.wait_recv()

        def collected(c):
            wanted = jnp.sum(in_ids[c], axis=0).astype(jnp.int32) - 1
            spread_out = (lax.broadcasted_iota(jnp.int32, (width, slots), 0) == wanted).astype(F32).astype(BF16)
            in_high, in_low = halves(in_rows[c])
            return halves(dot(spread_out, in_low) + dot(spread_out, in_high))

        @pl.when(cut == 0)
        def _():
            own[...] += dot3(collected(1), (own_high[...], own_low[...]))

        @pl.when(cut == 1)
        def _():
            own[...] += dot3((own_high[...], own_low[...]), collected(0), NT)

        own_high[...], own_low[...] = halves(own[...])
        for copy in to_host()[1:]:
            copy.wait_recv()
        chain_high[...], chain_low[...] = halves(env_far[...])

        @pl.when(cut == 0)
        def _():
            far[...] += dot3(collected(0), (chain_high[...], chain_low[...]))

        @pl.when(cut == 1)
        def _():
            far[...] += dot3((chain_high[...], chain_low[...]), collected(1), NT)


    def link(k):
        return remote(chunk(chain_out, k), chunk(chain_in, k), chain_send.at[k], chain_recv.at[k],
                      lax.rem(me + 2 * way + tiles, tiles), cut)

    def p_copy(k):
        return remote(chunk(chain_out, k), p_in, p_send.at[k], p_recv.at[0], k, 0)

    def q_along(i):
        return remote(part(q_in, i), part(q_in, i), q_send.at[0, i], q_recv.at[i], lax.rem(me + 2, tiles), cut)

    def q_across(i):
        return remote(part(q_in, i), part(q_in, i), q_send.at[1, i], q_recv.at[i], lax.rem(me + 1, tiles), cut)

    def q_half(i):
        return remote(part(chain_out, i), part(q_in, i), half_send.at[i], q_recv.at[i], 0, 0)

    even_tile = lax.rem(me, 2) == 0
    p_root = jnp.logical_and(last, cut == 0)
    q_root = jnp.logical_and(last, cut == 1)

    def emit(k, value):
        at = pl.ds(pl.multiple_of(k * step, 8), step)

        @pl.when(jnp.logical_not(last))
        def _():
            chain_out[at] = value
            link(k).start()

        @pl.when(p_root)
        def _():
            @pl.when(k < tiles - 1)
            def _():
                chain_out[at] = value
                p_copy(k).start()

            @pl.when(k == tiles - 1)
            def _():
                p_in[...] = value

        @pl.when(q_root)
        def _():
            @pl.when(k < pairs)
            def _():
                chain_out[at] = value
                for i in range(parts):
                    q_half(k * parts + i).start()

            @pl.when(k >= pairs)
            def _():
                q_in[pl.ds(pl.multiple_of((k - pairs) * step, 8), step)] = value
                for i in range(parts):
                    q_along((k - pairs) * parts + i).start()
                    q_across((k - pairs) * parts + i).start()

    @pl.when(place == 1)
    def _():
        @pl.loop(0, tiles)
        def _(k):
            at = pl.ds(pl.multiple_of(k * step, 8), step)
            emit(k, dot3(halves(far[at]), (own_high[...], own_low[...])))

    @pl.when(jnp.logical_and(host, place > 1))
    def _():
        chain_high[...], chain_low[...] = halves(dot3(halves(far[...]), (own_high[...], own_low[...])))

        @pl.loop(0, tiles)
        def _(k):
            at = pl.ds(pl.multiple_of(k * step, 8), step)
            link(k).wait_recv()
            emit(k, dot3(halves(chain_in[at]), (chain_high[...], chain_low[...])))

    @pl.when(jnp.logical_not(q_root))
    def _():
        @pl.loop(0, bits)
        def _(k):
            q_half(k).wait_recv()

            @pl.when(even_tile)
            def _():
                @pl.when(me < tiles - 2)
                def _():
                    q_along(k).start()

                q_across(k).start()

    def p_pass():
        return remote(p_in, p_in, pass_send.at[0], pass_recv.at[0], me, 1)

    @pl.when(cut == 0)
    def _():
        @pl.when(jnp.logical_not(p_root))
        def _():
            p_copy(0).wait_recv()

        p_pass().start()

    @pl.when(cut == 1)
    def _():
        p_pass().wait_recv()

    result = dot3(halves(p_in[...]), halves(q_in[...]), NT)
    block_ref[...] = result
    total = jnp.sum(jnp.sum(result * result, axis=0, keepdims=True), axis=1, keepdims=True)
    total = jnp.broadcast_to(total, (8, 128))
    sums_out[...] = total

    def share(peer, slot):
        return remote(sums_out, sums_in.at[slot], sum_send.at[peer], sum_recv.at[slot],
                      peer // 2, lax.rem(peer, 2))

    @pl.loop(1, count)
    def _(d):
        share(lax.rem(ident + d, count), ident).start()

    sums_in[ident] = total

    @pl.loop(1, pairs)
    def _(d):
        for copy in route(lax.rem(pair_me + d, pairs), me):
            copy.wait_send()

    @pl.when(jnp.logical_not(host))
    def _():
        for copy in route(pair_me, me) + to_host():
            copy.wait_send()

    @pl.when(jnp.logical_and(host, jnp.logical_not(last)))
    def _():
        @pl.loop(0, tiles)
        def _(k):
            link(k).wait_send()

    @pl.when(p_root)
    def _():
        @pl.loop(0, tiles - 1)
        def _(k):
            p_copy(k).wait_send()

    @pl.when(q_root)
    def _():
        @pl.loop(0, bits)
        def _(k):
            q_half(k).wait_send()

    @pl.when(even_tile)
    def _():
        @pl.loop(0, bits)
        def _(k):
            @pl.when(me < tiles - 2)
            def _():
                q_along(k).wait_send()

            q_across(k).wait_send()

    @pl.when(cut == 0)
    def _():
        p_pass().wait_send()

    @pl.loop(1, count)
    def _(d):
        peer = lax.rem(ident + d, count)
        share(peer, peer).wait_recv()
        share(peer, peer).wait_send()

    square_ref[...] = jnp.sum(sums_in[...], axis=0)


def body(slice_rows, row_owner, leaf_row, exponent, environment, ordering, sign_mask):
    tiles = lax.axis_size("tile")
    rows, width = slice_rows.shape
    step = width // tiles
    half = width // 2
    cap = max(2, (3 * rows + 2 * tiles - 1) // (2 * tiles))
    cap = (cap + 15) // 16 * 16
    slots = tiles * cap
    count = 2 * tiles
    parts = 4 if step % 64 == 0 else 1
    bits = tiles // 2 * parts
    vmem, dma = pltpu.VMEM, pltpu.SemaphoreType.DMA
    block, square = pl.pallas_call(
        functools.partial(kernel, tiles, cap, parts),
        out_shape=(jax.ShapeDtypeStruct((step, half), F32), jax.ShapeDtypeStruct((8, 128), F32)),
        in_specs=[pl.BlockSpec(memory_space=pl.ANY if i in (0, 4) else vmem) for i in range(7)],
        out_specs=(pl.BlockSpec(memory_space=vmem), pl.BlockSpec(memory_space=vmem)),
        scratch_shapes=[
            vmem((rows, width), F32), vmem((width, width), F32),
            vmem((tiles, cap, width), F32), vmem((tiles, 1, slots), F32),
            vmem((2, slots, width), F32), vmem((2, tiles, 1, slots), F32),
            vmem((2, width), jnp.int32), vmem((2, width), jnp.int32),
            vmem((width, width), F32), vmem((width, width), F32),
            vmem((width, width), F32), vmem((width, width), F32),
            vmem((width, width), BF16), vmem((width, width), BF16),
            vmem((width, width), BF16), vmem((width, width), BF16),
            vmem((width, width), F32), vmem((width, width), F32),
            vmem((step, width), F32), vmem((half, width), F32),
            vmem((8, 128), F32), vmem((count, 8, 128), F32),
            dma((2,)), dma((2, tiles // 2)), dma((2, tiles)), dma((3,)), dma((3,)), dma((tiles,)), dma((tiles,)),
            dma((tiles,)), dma((1,)), dma((1,)), dma((1,)),
            dma((2, bits)), dma((bits,)), dma((bits,)), dma((count,)), dma((count,)),
        ],
        compiler_params=pltpu.CompilerParams(
            collective_id=0, has_side_effects=True, vmem_limit_bytes=40 * 1024 * 1024),
    )(slice_rows, row_owner, leaf_row.reshape(1, rows), exponent.reshape(1, rows),
      environment, ordering, sign_mask)
    spread = jnp.sqrt(square[0, 0] / (width * width) + 1e-06)
    return block / spread, jnp.log(spread).reshape(1)


def from_partner(x, axis, bit):
    return lax.ppermute(x, axis, [(i, i ^ 1 << bit) for i in range(lax.axis_size(axis))])


def multiply(left_factor, right_factor):
    return jnp.dot(
        left_factor,
        right_factor,
        precision=lax.Precision.HIGHEST,
        preferred_element_type=jnp.float32,
    )


def plain_body(slice_rows, row_owner, leaf_row, exponent, environment, ordering, sign_mask):
    tiles = lax.axis_size("tile")
    cut_count = lax.axis_size("cuts")
    width = slice_rows.shape[1]
    row_count = slice_rows.shape[0]
    capacity = max(2, (3 * row_count + 2 * tiles - 1) // (2 * tiles))
    factor = jnp.where(exponent == -1, 0.5, jnp.where(exponent == 1, 2.0, 1.0)).astype(jnp.float32)
    scaled = slice_rows * factor[:, None]
    owners = row_owner[:, 0]
    hits = (owners[:, None] == jnp.arange(tiles, dtype=jnp.int32)[None, :]).astype(jnp.int32)
    before = jnp.cumsum(hits, axis=0) - hits
    position = jnp.sum(before * hits, axis=1)
    placed = owners * capacity + position
    outgoing = jnp.zeros((tiles * capacity, width), jnp.float32).at[placed].set(scaled)
    outgoing_rows = jnp.zeros((tiles * capacity,), jnp.int32).at[placed].set(leaf_row)
    arrived, arrived_rows = (
        lax.all_to_all(outgoing, "tile", split_axis=0, concat_axis=0, tiled=True),
        lax.all_to_all(outgoing_rows, "tile", split_axis=0, concat_axis=0, tiled=True),
    )
    collected = jnp.zeros((width, width), jnp.float32).at[arrived_rows].add(arrived)
    contracted = multiply(collected, environment)
    columns = jnp.arange(width, dtype=jnp.int32)
    signs = 1.0 - 2.0 * sign_mask[0].astype(jnp.float32)
    signed = (ordering[0][:, None] == columns[None, :]).astype(jnp.float32) * signs[:, None]
    product = contracted + signed
    for level in range(tiles.bit_length() - 1):
        partner = from_partner(product, "tile", level)
        upper = lax.axis_index("tile") >> level & 1 == 1
        first_part = jnp.where(upper, partner, product)
        second_part = jnp.where(upper, product, partner)
        product = multiply(first_part, second_part)
    level = 0
    partner = from_partner(product, "cuts", level)
    upper = lax.axis_index("cuts") >> level & 1 == 1
    first_part = jnp.where(upper, partner, product)
    second_part = jnp.where(upper, product, partner)
    product = multiply(first_part, second_part)
    spread = jnp.sqrt(jnp.mean(product * product) + 1e-06)
    rows_each = width // tiles
    cols_each = width // cut_count
    row_start = lax.axis_index("tile") * rows_each
    col_start = lax.axis_index("cuts") * cols_each
    own_block = lax.dynamic_slice(product, (row_start, col_start), (rows_each, cols_each))
    return (own_block / spread, jnp.log(spread).reshape(1))


def solution(mesh):
    tiles, cuts = mesh.shape["tile"], mesh.shape["cuts"]
    fits = cuts == 2 and 4 <= tiles <= 16
    return jax.shard_map(
        body if fits else plain_body,
        mesh=mesh,
        in_specs=(
            P(("groups", "tile", "cuts"), None),
            P(("groups", "tile", "cuts"), None),
            P(("groups", "tile", "cuts")),
            P(("groups", "tile", "cuts")),
            P(("groups", "tile", "cuts"), None),
            P(("groups", "tile", "cuts"), None),
            P(("groups", "tile", "cuts"), None),
        ),
        out_specs=(P(("groups", "tile"), "cuts"), P("groups")),
        check_vma=False,
    )
```

```python
import functools

import jax
import jax.numpy as jnp
from jax import lax
from jax.experimental import pallas as pl
from jax.experimental.pallas import tpu as pltpu
from jax.sharding import PartitionSpec as P

MESH = pl.DeviceIdType.MESH
F32, BF16 = jnp.float32, jnp.bfloat16
NN = (((1,), (0,)), ((), ()))
NT = (((1,), (1,)), ((), ()))


def halves(x):
    high = x.astype(BF16)
    return high, (x - high.astype(F32)).astype(BF16)


def dot(a, b, dims=NN):
    return lax.dot_general(a, b, dims, preferred_element_type=F32)


def dot3(left, right, dims=NN):
    return (dot(left[0], right[1], dims) + dot(left[1], right[0], dims)) + dot(left[0], right[0], dims)


def kernel(tiles, cap, parts,
           rows_ref, owner_ref, leaf_row_ref, exponent_ref, env_ref, ordering_ref, sign_ref,
           block_ref, square_ref,
           rows_in, env_in, out_rows, out_ids, in_rows, in_ids, bond_out, bond_in, env_out, env_far,
           own, far, own_high, own_low, chain_high, chain_low,
           chain_in, chain_out, p_in, q_in, sums_out, sums_in,
           load, route_send, route_recv, far_send, far_recv, chain_send, chain_recv,
           p_send, p_recv, pass_send, pass_recv, q_send, q_recv, half_send, sum_send, sum_recv):
    group, me, cut = lax.axis_index("groups"), lax.axis_index("tile"), lax.axis_index("cuts")
    load_env = pltpu.make_async_copy(env_ref, env_in, load.at[0])
    load_rows = pltpu.make_async_copy(rows_ref, rows_in, load.at[1])
    load_env.start()
    load_rows.start()
    rows, width = rows_ref.shape
    step = width // tiles
    pairs = tiles // 2
    bits = pairs * parts
    bit_rows = step // parts
    slots = tiles * cap
    count = 2 * tiles
    ident = me * 2 + cut
    place = jnp.where(cut == 0, me, tiles - 1 - me)
    way = 1 - 2 * cut
    last = place == tiles - 1
    host = lax.rem(place, 2) == 1
    pair_me = me // 2

    def chunk(ref, k):
        return ref.at[pl.ds(pl.multiple_of(k * step, 8), step)]

    def part(ref, i):
        return ref.at[pl.ds(pl.multiple_of(i * bit_rows, 8), bit_rows)]

    def remote(src, dst, send, recv, tile, other):
        return pltpu.make_async_remote_copy(
            src_ref=src, dst_ref=dst, send_sem=send, recv_sem=recv,
            device_id=(group, tile, other), device_id_type=MESH)

    barrier = pltpu.get_barrier_semaphore()

    @pl.loop(1, count)
    def _(d):
        peer = lax.rem(ident + d, count)
        pl.semaphore_signal(barrier, inc=1, device_id=(group, peer // 2, lax.rem(peer, 2)), device_id_type=MESH)

    bond_out[0:1] = ordering_ref[...]
    bond_out[1:2] = sign_ref[...]
    load_env.wait()

    @pl.when(cut == 0)
    def _():
        env_out[...] = env_in[...]

    @pl.when(cut == 1)
    def _():
        env_out[...] = env_in[...].T

    def to_host():
        to = lax.rem(me + way + tiles, tiles)
        return (remote(bond_out, bond_in, far_send.at[0], far_recv.at[0], to, cut),
                remote(env_out.at[:width // 2], env_far.at[:width // 2], far_send.at[1], far_recv.at[1], to, cut),
                remote(env_out.at[width // 2:], env_far.at[width // 2:], far_send.at[2], far_recv.at[2], to, cut))

    pl.semaphore_wait(barrier, count - 1)

    @pl.when(jnp.logical_not(host))
    def _():
        for copy in to_host()[:2]:
            copy.start()

    load_rows.wait()
    level = exponent_ref[...]
    factor = jnp.where(level == -1, 0.5, jnp.where(level == 1, 2.0, 1.0)).astype(F32)
    factor = jnp.broadcast_to(factor, (128, rows)).T[:, 0:1]
    scaled = rows_in[...] * factor
    owner = owner_ref[...]
    hits = (owner == lax.broadcasted_iota(jnp.int32, (rows, 128), 1)).astype(F32)
    earlier = (lax.broadcasted_iota(jnp.int32, (rows, rows), 1)
               < lax.broadcasted_iota(jnp.int32, (rows, rows), 0)).astype(F32)
    before = dot(earlier.astype(BF16), hits.astype(BF16))
    position = jnp.sum(before * hits, axis=1, keepdims=True)
    position = jnp.broadcast_to(position, (rows, 128)).T[0:1, :].astype(jnp.int32)
    owner = jnp.broadcast_to(owner.astype(F32), (rows, 128)).T[0:1, :].astype(jnp.int32)
    slot = lax.broadcasted_iota(jnp.int32, (slots, rows), 0)
    pick = (slot == owner * cap + position).astype(F32).astype(BF16)
    high = scaled.astype(BF16)
    rest = scaled - high.astype(F32)
    middle = rest.astype(BF16)
    low = (rest - middle.astype(F32)).astype(BF16)
    out_rows[...] = ((dot(pick, low) + dot(pick, middle)) + dot(pick, high)).reshape(tiles, cap, width)
    seat = (slot == me * cap + position).astype(F32).astype(BF16)
    named = jnp.where(lax.broadcasted_iota(jnp.int32, (tiles, rows), 0) == owner,
                      leaf_row_ref[...] + 1, 0).astype(F32)
    named_high, named_low = halves(named)
    ids = dot(named_high, seat, NT) + dot(named_low, seat, NT)
    for t in range(tiles):
        out_ids[t] = ids[t:t + 1, :]

    def slots_of(source):
        return pl.ds(pl.multiple_of(source * cap, 8), cap)

    def route(pair, source):
        both = pl.ds(2 * pair, 2)
        to = 2 * pair + 1 - cut
        return (remote(out_rows.at[both], in_rows.at[:, slots_of(source)], route_send.at[0, pair],
                       route_recv.at[0, source], to, cut),
                remote(out_ids.at[both], in_ids.at[:, source], route_send.at[1, pair],
                       route_recv.at[1, source], to, cut))

    @pl.loop(0, pairs)
    def _(d):
        pair = lax.rem(pair_me + pairs // 2 + d, pairs)

        @pl.when(pair != pair_me)
        def _():
            for copy in route(pair, me):
                copy.start()

    @pl.when(jnp.logical_not(host))
    def _():
        for copy in route(pair_me, me) + to_host()[2:]:
            copy.start()

    def bond_of(order, sign):
        return jnp.where(lax.broadcasted_iota(jnp.int32, (width, width), 0) == order,
                         (1 - 2 * sign).astype(F32), 0.0)

    @pl.when(host)
    def _():
        for c in range(2):
            in_rows[c, slots_of(me)] = out_rows[2 * pair_me + c]
            in_ids[c, me] = out_ids[2 * pair_me + c]
        to_host()[0].wait_recv()

        @pl.when(cut == 0)
        def _():
            own[...] = bond_of(bond_out[0:1], bond_out[1:2]).T
            far[...] = bond_of(bond_in[0:1], bond_in[1:2]).T

        @pl.when(cut == 1)
        def _():
            own[...] = bond_of(bond_out[0:1], bond_out[1:2])
            far[...] = bond_of(bond_in[0:1], bond_in[1:2])

        own_high[...], own_low[...] = halves(env_out[...])
        @pl.loop(1, tiles)
        def _(d):
            source = lax.rem(me + d, tiles)
            for copy in route(pair_me, source):
                copy.wait_recv()

        def collected(c):
            wanted = jnp.sum(in_ids[c], axis=0).astype(jnp.int32) - 1
            spread_out = (lax.broadcasted_iota(jnp.int32, (width, slots), 0) == wanted).astype(F32).astype(BF16)
            in_high, in_low = halves(in_rows[c])
            return halves(dot(spread_out, in_low) + dot(spread_out, in_high))

        @pl.when(cut == 0)
        def _():
            own[...] += dot3(collected(1), (own_high[...], own_low[...]))

        @pl.when(cut == 1)
        def _():
            own[...] += dot3((own_high[...], own_low[...]), collected(0), NT)

        own_high[...], own_low[...] = halves(own[...])
        for copy in to_host()[1:]:
            copy.wait_recv()
        chain_high[...], chain_low[...] = halves(env_far[...])

        @pl.when(cut == 0)
        def _():
            far[...] += dot3(collected(0), (chain_high[...], chain_low[...]))

        @pl.when(cut == 1)
        def _():
            far[...] += dot3((chain_high[...], chain_low[...]), collected(1), NT)


    def link(k):
        return remote(chunk(chain_out, k), chunk(chain_in, k), chain_send.at[k], chain_recv.at[k],
                      lax.rem(me + 2 * way + tiles, tiles), cut)

    def p_copy(k):
        return remote(chunk(chain_out, k), p_in, p_send.at[k], p_recv.at[0], k, 0)

    def q_along(i):
        return remote(part(q_in, i), part(q_in, i), q_send.at[0, i], q_recv.at[i], lax.rem(me + 2, tiles), cut)

    def q_across(i):
        return remote(part(q_in, i), part(q_in, i), q_send.at[1, i], q_recv.at[i], lax.rem(me + 1, tiles), cut)

    def q_half(i):
        return remote(part(chain_out, i), part(q_in, i), half_send.at[i], q_recv.at[i], 0, 0)

    even_tile = lax.rem(me, 2) == 0
    p_root = jnp.logical_and(last, cut == 0)
    q_root = jnp.logical_and(last, cut == 1)

    def emit(k, value):
        at = pl.ds(pl.multiple_of(k * step, 8), step)

        @pl.when(jnp.logical_not(last))
        def _():
            chain_out[at] = value
            link(k).start()

        @pl.when(p_root)
        def _():
            @pl.when(k < tiles - 1)
            def _():
                chain_out[at] = value
                p_copy(k).start()

            @pl.when(k == tiles - 1)
            def _():
                p_in[...] = value

        @pl.when(q_root)
        def _():
            @pl.when(k < pairs)
            def _():
                chain_out[at] = value
                for i in range(parts):
                    q_half(k * parts + i).start()

            @pl.when(k >= pairs)
            def _():
                q_in[pl.ds(pl.multiple_of((k - pairs) * step, 8), step)] = value
                for i in range(parts):
                    q_along((k - pairs) * parts + i).start()
                    q_across((k - pairs) * parts + i).start()

    @pl.when(place == 1)
    def _():
        @pl.loop(0, tiles)
        def _(k):
            at = pl.ds(pl.multiple_of(k * step, 8), step)
            emit(k, dot3(halves(far[at]), (own_high[...], own_low[...])))

    @pl.when(jnp.logical_and(host, place > 1))
    def _():
        chain_high[...], chain_low[...] = halves(dot3(halves(far[...]), (own_high[...], own_low[...])))

        @pl.loop(0, tiles)
        def _(k):
            at = pl.ds(pl.multiple_of(k * step, 8), step)
            link(k).wait_recv()
            emit(k, dot3(halves(chain_in[at]), (chain_high[...], chain_low[...])))

    @pl.when(jnp.logical_not(q_root))
    def _():
        @pl.loop(0, bits)
        def _(k):
            q_half(k).wait_recv()

            @pl.when(even_tile)
            def _():
                @pl.when(me < tiles - 2)
                def _():
                    q_along(k).start()

                q_across(k).start()

    def p_pass():
        return remote(p_in, p_in, pass_send.at[0], pass_recv.at[0], me, 1)

    @pl.when(cut == 0)
    def _():
        @pl.when(jnp.logical_not(p_root))
        def _():
            p_copy(0).wait_recv()

        p_pass().start()

    @pl.when(cut == 1)
    def _():
        p_pass().wait_recv()

    result = dot3(halves(p_in[...]), halves(q_in[...]), NT)
    block_ref[...] = result
    total = jnp.sum(jnp.sum(result * result, axis=0, keepdims=True), axis=1, keepdims=True)
    total = jnp.broadcast_to(total, (8, 128))
    sums_out[...] = total

    def share(peer, slot):
        return remote(sums_out, sums_in.at[slot], sum_send.at[peer], sum_recv.at[slot],
                      peer // 2, lax.rem(peer, 2))

    @pl.loop(1, count)
    def _(d):
        share(lax.rem(ident + d, count), ident).start()

    sums_in[ident] = total

    @pl.loop(1, pairs)
    def _(d):
        for copy in route(lax.rem(pair_me + d, pairs), me):
            copy.wait_send()

    @pl.when(jnp.logical_not(host))
    def _():
        for copy in route(pair_me, me) + to_host():
            copy.wait_send()

    @pl.when(jnp.logical_and(host, jnp.logical_not(last)))
    def _():
        @pl.loop(0, tiles)
        def _(k):
            link(k).wait_send()

    @pl.when(p_root)
    def _():
        @pl.loop(0, tiles - 1)
        def _(k):
            p_copy(k).wait_send()

    @pl.when(q_root)
    def _():
        @pl.loop(0, bits)
        def _(k):
            q_half(k).wait_send()

    @pl.when(even_tile)
    def _():
        @pl.loop(0, bits)
        def _(k):
            @pl.when(me < tiles - 2)
            def _():
                q_along(k).wait_send()

            q_across(k).wait_send()

    @pl.when(cut == 0)
    def _():
        p_pass().wait_send()

    @pl.loop(1, count)
    def _(d):
        peer = lax.rem(ident + d, count)
        share(peer, peer).wait_recv()
        share(peer, peer).wait_send()

    square_ref[...] = jnp.sum(sums_in[...], axis=0)


def body(slice_rows, row_owner, leaf_row, exponent, environment, ordering, sign_mask):
    tiles = lax.axis_size("tile")
    rows, width = slice_rows.shape
    step = width // tiles
    half = width // 2
    cap = max(2, (3 * rows + 2 * tiles - 1) // (2 * tiles))
    cap = (cap + 15) // 16 * 16
    slots = tiles * cap
    count = 2 * tiles
    parts = 4 if step % 64 == 0 else 1
    bits = tiles // 2 * parts
    vmem, dma = pltpu.VMEM, pltpu.SemaphoreType.DMA
    block, square = pl.pallas_call(
        functools.partial(kernel, tiles, cap, parts),
        out_shape=(jax.ShapeDtypeStruct((step, half), F32), jax.ShapeDtypeStruct((8, 128), F32)),
        in_specs=[pl.BlockSpec(memory_space=pl.ANY if i in (0, 4) else vmem) for i in range(7)],
        out_specs=(pl.BlockSpec(memory_space=vmem), pl.BlockSpec(memory_space=vmem)),
        scratch_shapes=[
            vmem((rows, width), F32), vmem((width, width), F32),
            vmem((tiles, cap, width), F32), vmem((tiles, 1, slots), F32),
            vmem((2, slots, width), F32), vmem((2, tiles, 1, slots), F32),
            vmem((2, width), jnp.int32), vmem((2, width), jnp.int32),
            vmem((width, width), F32), vmem((width, width), F32),
            vmem((width, width), F32), vmem((width, width), F32),
            vmem((width, width), BF16), vmem((width, width), BF16),
            vmem((width, width), BF16), vmem((width, width), BF16),
            vmem((width, width), F32), vmem((width, width), F32),
            vmem((step, width), F32), vmem((half, width), F32),
            vmem((8, 128), F32), vmem((count, 8, 128), F32),
            dma((2,)), dma((2, tiles // 2)), dma((2, tiles)), dma((3,)), dma((3,)), dma((tiles,)), dma((tiles,)),
            dma((tiles,)), dma((1,)), dma((1,)), dma((1,)),
            dma((2, bits)), dma((bits,)), dma((bits,)), dma((count,)), dma((count,)),
        ],
        compiler_params=pltpu.CompilerParams(
            collective_id=0, has_side_effects=True, vmem_limit_bytes=40 * 1024 * 1024),
    )(slice_rows, row_owner, leaf_row.reshape(1, rows), exponent.reshape(1, rows),
      environment, ordering, sign_mask)
    spread = jnp.sqrt(square[0, 0] / (width * width) + 1e-06)
    return block / spread, jnp.log(spread).reshape(1)


def from_partner(x, axis, bit):
    return lax.ppermute(x, axis, [(i, i ^ 1 << bit) for i in range(lax.axis_size(axis))])


def multiply(left_factor, right_factor):
    return jnp.dot(
        left_factor,
        right_factor,
        precision=lax.Precision.HIGHEST,
        preferred_element_type=jnp.float32,
    )


def plain_body(slice_rows, row_owner, leaf_row, exponent, environment, ordering, sign_mask):
    tiles = lax.axis_size("tile")
    cut_count = lax.axis_size("cuts")
    width = slice_rows.shape[1]
    row_count = slice_rows.shape[0]
    capacity = max(2, (3 * row_count + 2 * tiles - 1) // (2 * tiles))
    factor = jnp.where(exponent == -1, 0.5, jnp.where(exponent == 1, 2.0, 1.0)).astype(jnp.float32)
    scaled = slice_rows * factor[:, None]
    owners = row_owner[:, 0]
    hits = (owners[:, None] == jnp.arange(tiles, dtype=jnp.int32)[None, :]).astype(jnp.int32)
    before = jnp.cumsum(hits, axis=0) - hits
    position = jnp.sum(before * hits, axis=1)
    placed = owners * capacity + position
    outgoing = jnp.zeros((tiles * capacity, width), jnp.float32).at[placed].set(scaled)
    outgoing_rows = jnp.zeros((tiles * capacity,), jnp.int32).at[placed].set(leaf_row)
    arrived, arrived_rows = (
        lax.all_to_all(outgoing, "tile", split_axis=0, concat_axis=0, tiled=True),
        lax.all_to_all(outgoing_rows, "tile", split_axis=0, concat_axis=0, tiled=True),
    )
    collected = jnp.zeros((width, width), jnp.float32).at[arrived_rows].add(arrived)
    contracted = multiply(collected, environment)
    columns = jnp.arange(width, dtype=jnp.int32)
    signs = 1.0 - 2.0 * sign_mask[0].astype(jnp.float32)
    signed = (ordering[0][:, None] == columns[None, :]).astype(jnp.float32) * signs[:, None]
    product = contracted + signed
    for level in range(tiles.bit_length() - 1):
        partner = from_partner(product, "tile", level)
        upper = lax.axis_index("tile") >> level & 1 == 1
        first_part = jnp.where(upper, partner, product)
        second_part = jnp.where(upper, product, partner)
        product = multiply(first_part, second_part)
    level = 0
    partner = from_partner(product, "cuts", level)
    upper = lax.axis_index("cuts") >> level & 1 == 1
    first_part = jnp.where(upper, partner, product)
    second_part = jnp.where(upper, product, partner)
    product = multiply(first_part, second_part)
    spread = jnp.sqrt(jnp.mean(product * product) + 1e-06)
    rows_each = width // tiles
    cols_each = width // cut_count
    row_start = lax.axis_index("tile") * rows_each
    col_start = lax.axis_index("cuts") * cols_each
    own_block = lax.dynamic_slice(product, (row_start, col_start), (rows_each, cols_each))
    return (own_block / spread, jnp.log(spread).reshape(1))


def solution(mesh):
    tiles, cuts = mesh.shape["tile"], mesh.shape["cuts"]
    fits = cuts == 2 and 4 <= tiles <= 16
    return jax.shard_map(
        body if fits else plain_body,
        mesh=mesh,
        in_specs=(
            P(("groups", "tile", "cuts"), None),
            P(("groups", "tile", "cuts"), None),
            P(("groups", "tile", "cuts")),
            P(("groups", "tile", "cuts")),
            P(("groups", "tile", "cuts"), None),
            P(("groups", "tile", "cuts"), None),
            P(("groups", "tile", "cuts"), None),
        ),
        out_specs=(P(("groups", "tile"), "cuts"), P("groups")),
        check_vma=False,
    )
```
